256 devices in a mesh: section: 16 (over y, z_hi), res: 16 (over x, z_lo, core).
Axes of the slice: x: 4, y: 4, z: 8 (z_hi: 4, z_lo: 2; z = z_hi * 2 + z_lo), core: 2. Of those that a mesh axis runs over, the one named last changes fastest.
Arguments:
- normed_sequence_states: bfloat16 [16, 256, 128, 256], P('section', 'res'), may hold values from -6 to 6
- first_factor_tensor: bfloat16 [16, 256, 32], P('section'), may hold values from -0.375 to 0.375
- second_factor_tensor: bfloat16 [16, 256, 32], P('section'), may hold values from -0.375 to 0.375
- output_projection_weight: bfloat16 [16, 1024, 128], P('section'), may hold values from -0.1875 to 0.1875
- pair_external_gradient: bfloat16 [16, 256, 256, 128], P('section', 'res'), may hold values from -48 to 48
- pair_channel_gains: float32 [16, 128], P('section'), may hold values from 0.05 to 1
Outputs:
- msa_grad: bfloat16 [16, 256, 128, 256], P('section', 'res')
The draws below stay inside these ranges and needn't reach their ends.
All inputs are finite; a program needn't handle non-finite values.
Results may differ from the reference program's by a relative error of at most 0.02.
Values may be sent and summed in bfloat16 or wider, within the bound.
A program may use at most 192 MiB of HBM per device.

```python
import jax
import jax.numpy as jnp
from jax import lax

SEQUENCE_WIDTH = 256
PROJ_WIDTH_SIZE = 32
P_SIZE = 128
SEQUENCE_NUMBER = 128
POSITION_NUMBER = 256
TRUNK_DEPTH_SIZE = 16


def draw_pair_channel_gains(key, part):
    key = jax.random.fold_in(key, 7)
    variety_random_key, gradual_random_key, quick_random_key, spike_random_key, depth_random_key = jax.random.split(key, 5)
    slow_share = 0.5
    slow_low = 0.88
    kind_draw = jax.random.uniform(variety_random_key, (1, P_SIZE), jnp.float32)
    gradual_value = jax.random.uniform(gradual_random_key, (TRUNK_DEPTH_SIZE, P_SIZE), jnp.float32, slow_low, 1.0)
    fast_value = jax.random.uniform(quick_random_key, (TRUNK_DEPTH_SIZE, P_SIZE), jnp.float32, 0.05, 0.4)
    spike_sample = jax.random.uniform(spike_random_key, (TRUNK_DEPTH_SIZE, 1), jnp.float32)
    spike_depth = jax.random.uniform(depth_random_key, (TRUNK_DEPTH_SIZE, 1), jnp.float32, 0.5, 0.8)
    spike_multiplier = jnp.where(spike_sample < 0.2, spike_depth, 1.0)
    gradual_gain = gradual_value * spike_multiplier
    return jnp.where(kind_draw < slow_share, gradual_gain, fast_value).astype(jnp.float32)


def levels(key, dims, cuts, low, largest):
    factor_of, own = 1.0, jax.random.fold_in(key, 6)
    for dim, parts in cuts:
        steps = jnp.exp(jax.random.uniform(jax.random.fold_in(own, dim), (parts,), jnp.float32, low / len(cuts), largest / len(cuts)))
        factor_of = factor_of * jnp.repeat(steps, dims[dim] // parts).reshape([-1 if axis == dim else 1 for axis in range(len(dims))])
    return factor_of


def centred(own_key, dims, deviation, bound, cuts=(), dtype=jnp.bfloat16):
    factor_of = levels(own_key, dims, cuts, -0.22, 0.18) if cuts else 1.0
    array = jax.random.normal(own_key, dims, jnp.float32) * deviation * factor_of
    return jnp.minimum(jnp.maximum(array, -bound), bound).astype(dtype)


def setup_inputs(seed: int = 0) -> dict:
    keys = jax.random.split(jax.random.key(seed), 7)
    normed_sequence_states = centred(keys[0], (TRUNK_DEPTH_SIZE, POSITION_NUMBER, SEQUENCE_NUMBER, SEQUENCE_WIDTH), 1.0, 6.0, ((0, 16), (1, 16)))
    first_factor_tensor = centred(keys[1], (TRUNK_DEPTH_SIZE, SEQUENCE_WIDTH, PROJ_WIDTH_SIZE), SEQUENCE_WIDTH ** -0.5, 0.375, ((0, 16),))
    second_factor_tensor = centred(keys[2], (TRUNK_DEPTH_SIZE, SEQUENCE_WIDTH, PROJ_WIDTH_SIZE), SEQUENCE_WIDTH ** -0.5, 0.375, ((0, 16),))
    output_projection_weight = centred(keys[3], (TRUNK_DEPTH_SIZE, PROJ_WIDTH_SIZE * PROJ_WIDTH_SIZE, P_SIZE), (PROJ_WIDTH_SIZE * PROJ_WIDTH_SIZE) ** -0.5, 0.1875, ((0, 16),))
    pair_external_gradient = centred(keys[4], (TRUNK_DEPTH_SIZE, POSITION_NUMBER, POSITION_NUMBER, P_SIZE), 8.0, 48.0, ((0, 16), (1, 16)))
    pair_channel_gains = draw_pair_channel_gains(jax.random.fold_in(keys[6], 71), 0)
    return {"normed_sequence_states": normed_sequence_states, "first_factor_tensor": first_factor_tensor, "second_factor_tensor": second_factor_tensor, "output_projection_weight": output_projection_weight, "pair_external_gradient": pair_external_gradient, "pair_channel_gains": pair_channel_gains}


def block_gradient(call_arguments):
    normed_sequence_states, first_factor_tensor, second_factor_tensor, output_projection_weight, pair_gradient_total = call_arguments
    first_factor_vectors = jnp.einsum("egw,wa->eag", normed_sequence_states.astype(jnp.float32), first_factor_tensor.astype(jnp.float32)).astype(jnp.bfloat16)
    second_factor_vectors = jnp.einsum("egw,wa->eag", normed_sequence_states.astype(jnp.float32), second_factor_tensor.astype(jnp.float32)).astype(jnp.bfloat16)
    pair_half = pair_gradient_total.astype(jnp.bfloat16)
    incoming_adjoint = jnp.einsum("ijp,qp->ijq", pair_half.astype(jnp.float32), output_projection_weight.astype(jnp.float32)).astype(jnp.bfloat16)
    incoming_adjoint = incoming_adjoint.reshape(incoming_adjoint.shape[0], incoming_adjoint.shape[1], PROJ_WIDTH_SIZE, PROJ_WIDTH_SIZE).astype(jnp.float32)
    first_factor_adjoint = (jnp.einsum("zfay,fyb->zab", incoming_adjoint, second_factor_vectors.astype(jnp.float32)) / SEQUENCE_NUMBER).astype(jnp.bfloat16)
    second_factor_adjoint = (jnp.einsum("mvpg,mpw->vgw", incoming_adjoint, first_factor_vectors.astype(jnp.float32)) / SEQUENCE_NUMBER).astype(jnp.bfloat16)
    total = jnp.einsum("ixs,kx->isk", first_factor_adjoint.astype(jnp.float32), first_factor_tensor.astype(jnp.float32))
    total = total + jnp.einsum("ixs,kx->isk", second_factor_adjoint.astype(jnp.float32), second_factor_tensor.astype(jnp.float32))
    return total.astype(jnp.bfloat16)


def reference(normed_sequence_states, first_factor_tensor, second_factor_tensor, output_projection_weight, pair_external_gradient, pair_channel_gains):
    def chain_step(passed, inputs):
        grad_in, gains = inputs
        current = grad_in.astype(jnp.float32) + passed
        return gains[None, None, :] * current, current

    start_zero = jnp.zeros(pair_external_gradient.shape[1:], jnp.float32)
    _, pair_gradient_total = lax.scan(chain_step, start_zero, (pair_external_gradient, pair_channel_gains), reverse=True)
    return lax.map(block_gradient, (normed_sequence_states, first_factor_tensor, second_factor_tensor, output_projection_weight, pair_gradient_total))
```

```python
import jax
import jax.numpy as jnp
from jax import lax
from jax.experimental import pallas as pl
from jax.experimental.pallas import tpu as pltpu
from jax.sharding import PartitionSpec as P

MESH = pl.DeviceIdType.MESH
BF = jnp.bfloat16
F32 = jnp.float32
NSEC = 16
NRES = 16
ROWS = 16
SEQ = 128
CH = 256
W = 32
PC = 128
NX, NZ, NC = 4, 2, 2
JC = 128
YG = 4
YN = W // YG


def kernel(
    nrm_hbm, w1_hbm, w2_hbm, wout_hbm, pext_hbm, gain_hbm, out_hbm,
    nrm, w1, w2, wout, gain, gsend, gall,
    fr, bs, ph, wf, wp, lf, lt, rf, rall, osc, lacc, rg, c1, xs, xr, zs, zr, rgf, wt, outv,
    in_sem, gs_sem, gr_sem, fs_sem, fr_sem, bs_sem, br_sem, as_sem, ar_sem,
    cs_sem, cr_sem, xs_sem, xr_sem, zs_sem, zr_sem, out_sem,
):
    sec = lax.axis_index("section")
    res = lax.axis_index("res")
    mx, mz, mc = res // 4, lax.rem(res // 2, 2), lax.rem(res, 2)

    def at(x, z, c):
        return (sec, x * 4 + z * 2 + c)

    other_core = at(mx, mz, 1 - mc)
    other_z = at(mx, 1 - mz, mc)

    def x_peer(d):
        x = lax.rem(mx + d, NX)
        return x, at(x, mz, mc)

    loads = [
        pltpu.make_async_copy(src, dst, in_sem.at[n])
        for n, (src, dst) in enumerate(
            [(gain_hbm, gain), (nrm_hbm, nrm), (w1_hbm, w1), (w2_hbm, w2), (wout_hbm, wout)]
        )
    ]
    for load in loads:
        load.start()

    barrier = pltpu.get_barrier_semaphore()

    def greet(d, _):
        pl.semaphore_signal(
            barrier, inc=1, device_id=(lax.rem(sec + d, NSEC), res), device_id_type=MESH
        )
        return 0

    lax.fori_loop(1, NSEC, greet, 0)
    pl.semaphore_signal(barrier, inc=1, device_id=other_core, device_id_type=MESH)
    pl.semaphore_signal(barrier, inc=1, device_id=other_z, device_id_type=MESH)
    for d in range(1, NX):
        pl.semaphore_signal(barrier, inc=1, device_id=x_peer(d)[1], device_id_type=MESH)
    loads[0].wait()
    gsend[...] = jnp.broadcast_to(gain[...], gsend.shape)
    gall[sec] = gsend[...]
    pl.semaphore_wait(barrier, NSEC - 1 + 2 + NX - 1)

    def fwd(c, d):
        peer = lax.rem(sec + d, NSEC)
        return pltpu.make_async_remote_copy(
            src_ref=pext_hbm.at[peer, :, c],
            dst_ref=fr.at[c, sec],
            send_sem=fs_sem.at[c, d],
            recv_sem=fr_sem.at[c, sec],
            device_id=(peer, res),
            device_id_type=MESH,
        )

    def gains(d):
        peer = lax.rem(sec + d, NSEC)
        return pltpu.make_async_remote_copy(
            src_ref=gsend,
            dst_ref=gall.at[sec],
            send_sem=gs_sem.at[d],
            recv_sem=gr_sem.at[sec],
            device_id=(peer, res),
            device_id_type=MESH,
        )

    def own(c):
        return pltpu.make_async_copy(pext_hbm.at[sec, :, c], fr.at[c, sec], fr_sem.at[c, sec])

    def each(body, low=1, high=NSEC):
        def step(d, _):
            body(d)
            return 0

        lax.fori_loop(low, high, step, 0)

    each(lambda d: fwd(0, d).start())
    own(0).start()
    each(lambda d: gains(d).start())
    each(lambda d: fwd(1, d).start())
    own(1).start()

    loads[1].wait()
    loads[2].wait()
    loads[3].wait()
    wt[...] = jnp.concatenate([w1[...].astype(F32), w2[...].astype(F32)], axis=1).T.astype(BF)

    def project(n, _):
        block = nrm[pl.ds(n * 2, 2)].reshape(2 * SEQ, CH)
        both = lax.dot_general(
            wt[...], block, (((1,), (1,)), ((), ())), preferred_element_type=F32
        )
        for t in range(2):
            rows = pl.multiple_of((n * 2 + t) * W, W)
            lf[pl.ds(rows, W), :] = both[:W, t * SEQ : (t + 1) * SEQ]
            rf[pl.ds(rows, W), :] = both[W:, t * SEQ : (t + 1) * SEQ]
        return 0

    lax.fori_loop(0, ROWS // 2, project, 0)
    for y in range(W):
        rall[mx, mz, mc, y] = rf[pl.ds(y, ROWS, stride=W), :].astype(BF)

    def share(n, x, z, c, to):
        return pltpu.make_async_remote_copy(
            src_ref=rall.at[x, z, c],
            dst_ref=rall.at[x, z, c],
            send_sem=as_sem.at[n],
            recv_sem=ar_sem.at[x, z, c],
            device_id=to,
            device_id_type=MESH,
        )

    def arrived(x, z, c):
        pltpu.make_async_copy(rall.at[x, z, c], rall.at[x, z, c], ar_sem.at[x, z, c]).wait()

    shares = [share(0, mx, mz, mc, other_z)]
    shares += [share(d, mx, mz, mc, x_peer(d)[1]) for d in range(1, NX)]
    shares += [share(4, mx, mz, mc, other_core)]
    for copy in shares:
        copy.start()

    for n in range(4):
        lt[:, n * 128 : (n + 1) * 128] = lf[n * 128 : (n + 1) * 128, :].T.astype(BF)
    loads[4].wait()
    wf[...] = wout[...].astype(F32)
    for y in range(W):
        wp[y * W : (y + 1) * W, :] = wf[pl.ds(y, W, stride=W), :].astype(BF)
    lacc[...] = jnp.zeros_like(lacc)

    arrived(mx, 1 - mz, mc)
    more = [share(4 + d, mx, 1 - mz, mc, x_peer(d)[1]) for d in range(1, NX)]
    more += [share(8, mx, 1 - mz, mc, other_core)]
    for copy in more:
        copy.start()
    shares += more
    for d in range(1, NX):
        x = x_peer(d)[0]
        for z in (0, 1):
            arrived(x, z, mc)
            copy = share(7 + 2 * d + z, x, z, mc, other_core)
            copy.start()
            shares.append(copy)

    def back(c, d):
        peer = lax.rem(sec + d, NSEC)
        return pltpu.make_async_remote_copy(
            src_ref=bs.at[c, peer],
            dst_ref=ph.at[c, sec],
            send_sem=bs_sem.at[c, d],
            recv_sem=br_sem.at[c, sec],
            device_id=(peer, res),
            device_id_type=MESH,
        )

    def gain_arrived(d):
        k = lax.rem(sec + d, NSEC)
        pltpu.make_async_copy(gall.at[k], gall.at[k], gr_sem.at[k]).wait()

    def scan(c):
        if c == 0:
            each(gain_arrived)
        each(lambda k: pltpu.make_async_copy(fr.at[c, k], fr.at[c, k], fr_sem.at[c, k]).wait(), 0)

        def block(n, _):
            total = None
            for k in range(NSEC - 1, -1, -1):
                grad = fr[c, k, n].astype(F32)
                total = grad if total is None else grad + gall[k + 1, 0:1, :] * total
                bs[c, k, n] = total.astype(BF)
            return 0

        lax.fori_loop(0, NX, block, 0)
        pltpu.make_async_copy(bs.at[c, sec], ph.at[c, sec], br_sem.at[c, sec]).start()
        each(lambda d: back(c, d).start())

    def chunk(c):
        each(lambda k: pltpu.make_async_copy(ph.at[c, k], ph.at[c, k], br_sem.at[c, k]).wait(), 0)

        def outer(n, _):
            pair = ph[c, pl.ds(n * 2, 2)].reshape(2 * JC, PC)
            grad = lax.dot_general(
                wp[...], pair, (((1,), (1,)), ((), ())), preferred_element_type=F32
            ).astype(BF)
            for t in range(2):
                osc[n * 2 + t] = grad[:, t * JC : (t + 1) * JC].reshape(W, W, JC)
            return 0

        lax.fori_loop(0, ROWS // 2, outer, 0)

        def two(y):
            return jnp.concatenate(
                [osc[:, y + t].reshape(ROWS * W, JC) for t in range(2)], axis=1
            )

        def core_copy(g):
            ys = pl.ds(g * YN, YN)
            return pltpu.make_async_remote_copy(
                src_ref=rg.at[c, 1 - mc, :, ys],
                dst_ref=c1.at[c, :, ys],
                send_sem=cs_sem.at[c, g],
                recv_sem=cr_sem.at[c, g],
                device_id=other_core,
                device_id_type=MESH,
            )

        for g in range(YG):

            def right(n, _):
                y = g * YN + n * 2
                grad = jnp.dot(lt[...], two(y), preferred_element_type=F32)
                for t in range(2):
                    turned = grad[:, t * JC : (t + 1) * JC].T.astype(BF)
                    turned = turned.reshape(NX, NC, ROWS, SEQ)
                    for core in range(NC):
                        rg[c, core, :, y + t] = turned[:, core]
                return 0

            lax.fori_loop(0, YN // 2, right, 0)
            core_copy(g).start()

        def x_copy(g, d):
            ys = pl.ds(g * YN, YN)
            x, peer = x_peer(d)
            return pltpu.make_async_remote_copy(
                src_ref=xs.at[c, x, ys],
                dst_ref=xr.at[c, mx, ys],
                send_sem=xs_sem.at[c, g, d],
                recv_sem=xr_sem.at[c, g, mx],
                device_id=peer,
                device_id_type=MESH,
            )

        for g in range(YG):
            core_copy(g).wait_recv()

            def add_core(n, _):
                y = g * YN + n
                xs[c, :, y] = (
                    rg[c, mc, :, y].astype(F32) + c1[c, :, y].astype(F32)
                ).astype(BF)
                return 0

            lax.fori_loop(0, YN, add_core, 0)
            for d in range(1, NX):
                x_copy(g, d).start()

        def left(n, _):
            ys = n * 8
            terms = jnp.concatenate(
                [osc[:, ys + t].reshape(ROWS * W, JC) for t in range(8)], axis=1
            )
            vectors = jnp.concatenate(
                [rall[:, c, :, ys + t].reshape(JC, SEQ) for t in range(8)], axis=0
            )
            lacc[...] += jnp.dot(terms, vectors, preferred_element_type=F32)
            return 0

        if c == 0:
            for x in range(NX):
                for z in range(NZ):
                    arrived(x, z, 1 - mc)
        lax.fori_loop(0, W // 8, left, 0)

        def z_copy(g):
            ys = pl.ds(g * YN, YN)
            return pltpu.make_async_remote_copy(
                src_ref=zs.at[c, ys],
                dst_ref=zr.at[c, ys],
                send_sem=zs_sem.at[c, g],
                recv_sem=zr_sem.at[c, g],
                device_id=other_z,
                device_id_type=MESH,
            )

        for g in range(YG):
            for d in range(1, NX):
                x = x_peer(d)[0]
                part = xr.at[c, x, pl.ds(g * YN, YN)]
                pltpu.make_async_copy(part, part, xr_sem.at[c, g, x]).wait()

            def add_x(n, _):
                y = g * YN + n
                total = xs[c, mx, y].astype(F32)
                for d in range(1, NX):
                    total += xr[c, x_peer(d)[0], y].astype(F32)
                zs[c, y] = total.astype(BF)
                return 0

            lax.fori_loop(0, YN, add_x, 0)

            @pl.when(mz != c)
            def _():
                z_copy(g).start()

        @pl.when(mz == c)
        def _():
            for g in range(YG):
                z_copy(g).wait_recv()

                def add_z(n, _):
                    y = g * YN + n
                    rows = pl.multiple_of(y * ROWS, ROWS)
                    rgf[pl.ds(rows, ROWS), :] = zs[c, y].astype(F32) + zr[c, y].astype(F32)
                    return 0

                lax.fori_loop(0, YN, add_z, 0)

        def finish():
            for g in range(YG):
                core_copy(g).wait_send()
                for d in range(1, NX):
                    x_copy(g, d).wait_send()

            @pl.when(mz != c)
            def _():
                for g in range(YG):
                    z_copy(g).wait_send()

        return finish

    scan(0)
    scan(1)
    end0 = chunk(0)
    end1 = chunk(1)

    for i in range(ROWS):
        both = jnp.concatenate(
            [lacc[i * W : (i + 1) * W, :], rgf[pl.ds(i, W, stride=ROWS), :]], axis=0
        )
        both = (both * (1.0 / SEQ)).astype(BF)
        outv[i] = lax.dot_general(
            both, wt[...], (((0,), (0,)), ((), ())), preferred_element_type=F32
        ).astype(BF)
    done = pltpu.make_async_copy(outv, out_hbm, out_sem)
    done.start()

    for c in range(2):
        each(lambda d: fwd(c, d).wait_send())
        each(lambda d: back(c, d).wait_send())
    each(lambda d: gains(d).wait_send())
    for copy in shares:
        copy.wait_send()
    end0()
    end1()
    done.wait()


def shards(nrm, w1, w2, wout, pext, gain):
    anyspace = pl.BlockSpec(memory_space=pl.ANY)
    vm = pltpu.VMEM
    dma = pltpu.SemaphoreType.DMA
    out = pl.pallas_call(
        kernel,
        out_shape=jax.ShapeDtypeStruct((ROWS, SEQ, CH), BF),
        in_specs=[anyspace] * 6,
        out_specs=anyspace,
        scratch_shapes=[
            vm((ROWS, SEQ, CH), BF),
            vm((CH, W), BF),
            vm((CH, W), BF),
            vm((W * W, PC), BF),
            vm((1, PC), F32),
            vm((8, PC), F32),
            vm((NSEC, 8, PC), F32),
            vm((2, NSEC, NX, JC // NX, PC), BF),
            vm((2, NSEC, NX, JC // NX, PC), BF),
            vm((2, NSEC, NX, JC // NX, PC), BF),
            vm((W * W, PC), F32),
            vm((W * W, PC), BF),
            vm((ROWS * W, SEQ), F32),
            vm((SEQ, ROWS * W), BF),
            vm((ROWS * W, SEQ), F32),
            vm((NX, NZ, NC, W, ROWS, SEQ), BF),
            vm((ROWS, W, W, JC), BF),
            vm((ROWS * W, SEQ), F32),
            vm((2, NC, NX, W, ROWS, SEQ), BF),
            vm((2, NX, W, ROWS, SEQ), BF),
            vm((2, NX, W, ROWS, SEQ), BF),
            vm((2, NX, W, ROWS, SEQ), BF),
            vm((2, W, ROWS, SEQ), BF),
            vm((2, W, ROWS, SEQ), BF),
            vm((W * ROWS, SEQ), F32),
            vm((2 * W, CH), BF),
            vm((ROWS, SEQ, CH), BF),
            dma((5,)),
            dma((NSEC,)),
            dma((NSEC,)),
            dma((2, NSEC)),
            dma((2, NSEC)),
            dma((2, NSEC)),
            dma((2, NSEC)),
            dma((16,)),
            dma((NX, NZ, NC)),
            dma((2, YG)),
            dma((2, YG)),
            dma((2, YG, NX)),
            dma((2, YG, NX)),
            dma((2, YG)),
            dma((2, YG)),
            dma,
        ],
        compiler_params=pltpu.CompilerParams(
            collective_id=0, has_side_effects=True, vmem_limit_bytes=56 << 20
        ),
        cost_estimate=pl.CostEstimate(
            flops=3_400_000_000, bytes_accessed=4 << 20, transcendentals=0
        ),
        name="fused",
    )(
        nrm[0],
        w1[0],
        w2[0],
        wout[0],
        pext[0].reshape(ROWS, NX, NZ, JC // NX, PC),
        gain,
    )
    return out[None]


def solution(mesh):
    in_specs = (
        P("section", "res", None, None),
        P("section", None, None),
        P("section", None, None),
        P("section", None, None),
        P("section", "res", None, None),
        P("section", None),
    )
    out_specs = P("section", "res", None, None)
    return jax.shard_map(shards, mesh=mesh, in_specs=in_specs, out_specs=out_specs, check_vma=False)
```

```python
import jax
import jax.numpy as jnp
from jax import lax
from jax.experimental import pallas as pl
from jax.experimental.pallas import tpu as pltpu
from jax.sharding import PartitionSpec as P

MESH = pl.DeviceIdType.MESH
BF = jnp.bfloat16
F32 = jnp.float32
NSEC = 16
NRES = 16
ROWS = 16
SEQ = 128
CH = 256
W = 32
PC = 128
NX, NZ, NC = 4, 2, 2
NQ = NZ * NC
JC = NX * ROWS
YP = W // 2
YG = 2
YN = W // YG


def kernel(
    nrm_hbm, w1_hbm, w2_hbm, wout_hbm, pext_hbm, gain_hbm, out_hbm,
    nrm, w1, w2, wout, gain, gsend, gall,
    fr, bs, ph, wf, wp, lf, lt, rf, rall, osc, lacc, rg, c1, xs, xr, zs, zr, rgf, wt, outv,
    in_sem, gs_sem, gr_sem, fs_sem, fr_sem, bs_sem, br_sem, as_sem, ar_sem,
    cs_sem, cr_sem, xs_sem, xr_sem, zs_sem, zr_sem, out_sem,
):
    sec = lax.axis_index("section")
    res = lax.axis_index("res")
    mx, mz, mc = res // 4, lax.rem(res // 2, 2), lax.rem(res, 2)

    def at(x, z, c):
        return (sec, x * 4 + z * 2 + c)

    other_core = at(mx, mz, 1 - mc)
    other_z = at(mx, 1 - mz, mc)

    def x_peer(d):
        x = lax.rem(mx + d, NX)
        return x, at(x, mz, mc)

    loads = [
        pltpu.make_async_copy(src, dst, in_sem.at[n])
        for n, (src, dst) in enumerate(
            [(gain_hbm, gain), (nrm_hbm, nrm), (w1_hbm, w1), (w2_hbm, w2), (wout_hbm, wout)]
        )
    ]
    for load in loads:
        load.start()

    barrier = pltpu.get_barrier_semaphore()

    def greet(d, _):
        pl.semaphore_signal(
            barrier, inc=1, device_id=(lax.rem(sec + d, NSEC), res), device_id_type=MESH
        )
        return 0

    lax.fori_loop(1, NSEC, greet, 0)
    pl.semaphore_signal(barrier, inc=1, device_id=other_core, device_id_type=MESH)
    pl.semaphore_signal(barrier, inc=1, device_id=other_z, device_id_type=MESH)
    for d in range(1, NX):
        pl.semaphore_signal(barrier, inc=1, device_id=x_peer(d)[1], device_id_type=MESH)
    loads[0].wait()
    gsend[...] = jnp.broadcast_to(gain[...], gsend.shape)
    gall[sec] = gsend[...]
    pl.semaphore_wait(barrier, NSEC - 1 + 2 + NX - 1)

    def fwd(c, d):
        peer = lax.rem(sec + d, NSEC)
        return pltpu.make_async_remote_copy(
            src_ref=pext_hbm.at[peer, :, c],
            dst_ref=fr.at[c, sec],
            send_sem=fs_sem.at[c, d],
            recv_sem=fr_sem.at[c, sec],
            device_id=(peer, res),
            device_id_type=MESH,
        )

    def gains(d):
        peer = lax.rem(sec + d, NSEC)
        return pltpu.make_async_remote_copy(
            src_ref=gsend,
            dst_ref=gall.at[sec],
            send_sem=gs_sem.at[d],
            recv_sem=gr_sem.at[sec],
            device_id=(peer, res),
            device_id_type=MESH,
        )

    def each(body, low=1, high=NSEC):
        def step(d, _):
            body(d)
            return 0

        lax.fori_loop(low, high, step, 0)

    def send_fwd(c):
        each(lambda d: fwd(c, d).start())
        pltpu.make_async_copy(pext_hbm.at[sec, :, c], fr.at[c, sec], fr_sem.at[c, sec]).start()

    send_fwd(0)
    each(lambda d: gains(d).start())
    send_fwd(1)

    loads[1].wait()
    loads[2].wait()
    loads[3].wait()
    wt[:W] = w1[...]
    wt[W:] = w2[...]

    def project(n, _):
        block = nrm[pl.ds(n * 2, 2)].reshape(2 * SEQ, CH)
        both = lax.dot_general(
            wt[...], block, (((1,), (1,)), ((), ())), preferred_element_type=F32
        )
        for t in range(2):
            rows = pl.multiple_of((n * 2 + t) * W, W)
            lf[pl.ds(rows, W), :] = both[:W, t * SEQ : (t + 1) * SEQ]
            rf[pl.ds(rows, W), :] = both[W:, t * SEQ : (t + 1) * SEQ]
        return 0

    lax.fori_loop(0, ROWS // 2, project, 0)
    for y in range(W):
        rall[mx, mz, mc, y] = rf[pl.ds(y, ROWS, stride=W), :].astype(BF)

    def share(n, x, z, c, to):
        return pltpu.make_async_remote_copy(
            src_ref=rall.at[x, z, c],
            dst_ref=rall.at[x, z, c],
            send_sem=as_sem.at[n],
            recv_sem=ar_sem.at[x, z, c],
            device_id=to,
            device_id_type=MESH,
        )

    def arrived(x, z, c):
        pltpu.make_async_copy(rall.at[x, z, c], rall.at[x, z, c], ar_sem.at[x, z, c]).wait()

    shares = []

    def pass_on(copies):
        for copy in copies:
            copy.start()
        shares.extend(copies)

    pass_on(
        [share(0, mx, mz, mc, other_z)]
        + [share(d, mx, mz, mc, x_peer(d)[1]) for d in range(1, NX)]
        + [share(4, mx, mz, mc, other_core)]
    )
    send_fwd(2)
    send_fwd(3)

    for n in range(4):
        lt[:, n * 128 : (n + 1) * 128] = lf[n * 128 : (n + 1) * 128, :].T.astype(BF)
    loads[4].wait()
    wf[...] = wout[...].astype(F32)
    for y in range(W):
        wp[(y // 2) * W : (y // 2 + 1) * W, (y % 2) * PC : (y % 2 + 1) * PC] = wf[
            pl.ds(y, W, stride=W), :
        ].astype(BF)
    lacc[...] = jnp.zeros_like(lacc)

    def pass_z():
        arrived(mx, 1 - mz, mc)
        pass_on(
            [share(4 + d, mx, 1 - mz, mc, x_peer(d)[1]) for d in range(1, NX)]
            + [share(8, mx, 1 - mz, mc, other_core)]
        )

    def pass_x(n):
        for d in range(1, NX):
            x = x_peer(d)[0]
            z = mz if n == 0 else 1 - mz
            arrived(x, z, mc)
            pass_on([share(7 + 2 * d + n, x, z, mc, other_core)])

    def back(c, d):
        peer = lax.rem(sec + d, NSEC)
        return pltpu.make_async_remote_copy(
            src_ref=bs.at[c, peer],
            dst_ref=ph.at[c, sec],
            send_sem=bs_sem.at[c, d],
            recv_sem=br_sem.at[c, sec],
            device_id=(peer, res),
            device_id_type=MESH,
        )

    def gain_arrived(d):
        k = lax.rem(sec + d, NSEC)
        pltpu.make_async_copy(gall.at[k], gall.at[k], gr_sem.at[k]).wait()

    def scan(c):
        if c == 0:
            each(gain_arrived)
        each(lambda k: pltpu.make_async_copy(fr.at[c, k], fr.at[c, k], fr_sem.at[c, k]).wait(), 0)
        total = None
        for k in range(NSEC - 1, -1, -1):
            grad = fr[c, k].reshape(JC, PC).astype(F32)
            total = grad if total is None else grad + gall[k + 1, 0:1, :] * total
            bs[c, k] = total.astype(BF).reshape(NX, ROWS, PC)
        pltpu.make_async_copy(bs.at[c, sec], ph.at[c, sec], br_sem.at[c, sec]).start()
        each(lambda d: back(c, d).start())

    def core_copy(c, g):
        ys = pl.ds(g * YN, YN)
        return pltpu.make_async_remote_copy(
            src_ref=rg.at[c, :, ys],
            dst_ref=c1.at[c // 2, :, ys],
            send_sem=cs_sem.at[c, g],
            recv_sem=cr_sem.at[c // 2, g],
            device_id=other_core,
            device_id_type=MESH,
        )

    def x_copy(c, g, d):
        ys = pl.ds(g * YN, YN)
        x, peer = x_peer(d)
        return pltpu.make_async_remote_copy(
            src_ref=xs.at[c // 2, x, ys],
            dst_ref=xr.at[c // 2, mx, ys],
            send_sem=xs_sem.at[c // 2, g, d],
            recv_sem=xr_sem.at[c // 2, g, mx],
            device_id=peer,
            device_id_type=MESH,
        )

    def z_copy(g):
        ys = pl.ds(g * YN, YN)
        return pltpu.make_async_remote_copy(
            src_ref=zs.at[1 - mz, ys],
            dst_ref=zr.at[ys],
            send_sem=zs_sem.at[g],
            recv_sem=zr_sem.at[g],
            device_id=other_z,
            device_id_type=MESH,
        )

    def products(c):
        def outer(n, _):
            wide = []
            for t in range(2):
                i = lax.rem(sec - n * 2 - t + NSEC, NSEC)
                pltpu.make_async_copy(ph.at[c, i], ph.at[c, i], br_sem.at[c, i]).wait()
                pair = ph[c, i].reshape(JC, PC)
                none = jnp.zeros_like(pair)
                wide += [
                    jnp.concatenate([pair, none], axis=1),
                    jnp.concatenate([none, pair], axis=1),
                ]
            grad = lax.dot_general(
                wp[...],
                jnp.concatenate(wide, axis=0),
                (((1,), (1,)), ((), ())),
                preferred_element_type=F32,
            ).astype(BF)
            for t in range(2):
                i = lax.rem(sec - n * 2 - t + NSEC, NSEC)
                osc[i] = grad[:, t * 2 * JC : (t + 1) * 2 * JC].reshape(YP, W, 2 * JC)
            return 0

        lax.fori_loop(0, ROWS // 2, outer, 0)

        for g in range(YG):

            def right(n, _):
                yp = g * (YN // 2) + n * 2
                both = jnp.concatenate(
                    [osc[:, yp + t].reshape(ROWS * W, 2 * JC) for t in range(2)], axis=1
                )
                grad = jnp.dot(lt[...], both, preferred_element_type=F32)
                for t in range(2):
                    turned = grad[:, t * 2 * JC : (t + 1) * 2 * JC].T.astype(BF)
                    turned = turned.reshape(2, NX, ROWS, SEQ)
                    for u in range(2):
                        rg[c, :, (yp + t) * 2 + u] = turned[u]
                return 0

            lax.fori_loop(0, YN // 4, right, 0)

            @pl.when(mc != c % 2)
            def _():
                core_copy(c, g).start()

        def left(n, _):
            terms = jnp.concatenate(
                [osc[:, n * 8 + t].reshape(ROWS * W, 2 * JC) for t in range(8)], axis=1
            )
            vectors = jnp.concatenate(
                [rall[:, c // 2, c % 2, n * 16 + t].reshape(JC, SEQ) for t in range(16)], axis=0
            )
            lacc[...] += jnp.dot(terms, vectors, preferred_element_type=F32)
            return 0

        lax.fori_loop(0, YP // 8, left, 0)

    def over_cores(c):
        @pl.when(mc == c % 2)
        def _():
            for g in range(YG):
                core_copy(c, g).wait_recv()

                def add_core(n, _):
                    y = g * YN + n
                    xs[c // 2, :, y] = (
                        rg[c, :, y].astype(F32) + c1[c // 2, :, y].astype(F32)
                    ).astype(BF)
                    return 0

                lax.fori_loop(0, YN, add_core, 0)
                for d in range(1, NX):
                    x_copy(c, g, d).start()

    def over_x(c):
        @pl.when(mc == c % 2)
        def _():
            for g in range(YG):
                for d in range(1, NX):
                    x = x_peer(d)[0]
                    part = xr.at[c // 2, x, pl.ds(g * YN, YN)]
                    pltpu.make_async_copy(part, part, xr_sem.at[c // 2, g, x]).wait()

                def add_x(n, _):
                    y = g * YN + n
                    total = xs[c // 2, mx, y].astype(F32)
                    for d in range(1, NX):
                        total += xr[c // 2, x_peer(d)[0], y].astype(F32)
                    zs[c // 2, y] = total.astype(BF)
                    return 0

                lax.fori_loop(0, YN, add_x, 0)

                @pl.when(mz != c // 2)
                def _():
                    z_copy(g).start()

    def over_z():
        for g in range(YG):
            z_copy(g).wait_recv()

            def add_z(n, _):
                y = g * YN + n
                rows = pl.multiple_of(y * ROWS, ROWS)
                rgf[pl.ds(rows, ROWS), :] = zs[mz, y].astype(F32) + zr[y].astype(F32)
                return 0

            lax.fori_loop(0, YN, add_z, 0)

    pass_z()
    scan(0)
    pass_x(0)
    scan(1)
    pass_x(1)
    scan(2)
    scan(3)
    for x in range(NX):
        for z in range(NZ):
            arrived(x, z, 1 - mc)
    for c in range(NQ):
        products(c)
        if c:
            over_x(c - 1)
        over_cores(c)
    over_x(NQ - 1)
    over_z()

    for i in range(ROWS):
        both = jnp.concatenate(
            [lacc[i * W : (i + 1) * W, :], rgf[pl.ds(i, W, stride=ROWS), :]], axis=0
        )
        both = (both * (1.0 / SEQ)).astype(BF)
        outv[i] = lax.dot_general(
            both, wt[...], (((0,), (0,)), ((), ())), preferred_element_type=F32
        ).astype(BF)
    done = pltpu.make_async_copy(outv, out_hbm, out_sem)
    done.start()

    for c in range(NQ):
        each(lambda d: fwd(c, d).wait_send())
        each(lambda d: back(c, d).wait_send())
    each(lambda d: gains(d).wait_send())
    for copy in shares:
        copy.wait_send()
    for c in range(NQ):
        for g in range(YG):

            @pl.when(mc != c % 2)
            def _():
                core_copy(c, g).wait_send()

            @pl.when(mc == c % 2)
            def _():
                for d in range(1, NX):
                    x_copy(c, g, d).wait_send()

    for g in range(YG):
        z_copy(g).wait_send()
    done.wait()


def shards(nrm, w1, w2, wout, pext, gain):
    anyspace = pl.BlockSpec(memory_space=pl.ANY)
    vm = pltpu.VMEM
    dma = pltpu.SemaphoreType.DMA
    out = pl.pallas_call(
        kernel,
        out_shape=jax.ShapeDtypeStruct((ROWS, SEQ, CH), BF),
        in_specs=[anyspace] * 6,
        out_specs=anyspace,
        scratch_shapes=[
            vm((ROWS, SEQ, CH), BF),
            vm((W, CH), BF),
            vm((W, CH), BF),
            vm((W * W, PC), BF),
            vm((1, PC), F32),
            vm((8, PC), F32),
            vm((NSEC, 8, PC), F32),
            vm((NQ, NSEC, NX, ROWS, PC), BF),
            vm((NQ, NSEC, NX, ROWS, PC), BF),
            vm((NQ, NSEC, NX, ROWS, PC), BF),
            vm((W * W, PC), F32),
            vm((YP * W, 2 * PC), BF),
            vm((ROWS * W, SEQ), F32),
            vm((SEQ, ROWS * W), BF),
            vm((ROWS * W, SEQ), F32),
            vm((NX, NZ, NC, W, ROWS, SEQ), BF),
            vm((ROWS, YP, W, 2 * JC), BF),
            vm((ROWS * W, SEQ), F32),
            vm((NQ, NX, W, ROWS, SEQ), BF),
            vm((2, NX, W, ROWS, SEQ), BF),
            vm((2, NX, W, ROWS, SEQ), BF),
            vm((2, NX, W, ROWS, SEQ), BF),
            vm((2, W, ROWS, SEQ), BF),
            vm((W, ROWS, SEQ), BF),
            vm((W * ROWS, SEQ), F32),
            vm((2 * W, CH), BF),
            vm((ROWS, SEQ, CH), BF),
            dma((5,)),
            dma((NSEC,)),
            dma((NSEC,)),
            dma((NQ, NSEC)),
            dma((NQ, NSEC)),
            dma((NQ, NSEC)),
            dma((NQ, NSEC)),
            dma((16,)),
            dma((NX, NZ, NC)),
            dma((NQ, YG)),
            dma((NZ, YG)),
            dma((NZ, YG, NX)),
            dma((NZ, YG, NX)),
            dma((YG,)),
            dma((YG,)),
            dma,
        ],
        compiler_params=pltpu.CompilerParams(
            collective_id=0, has_side_effects=True, vmem_limit_bytes=56 << 20
        ),
        cost_estimate=pl.CostEstimate(
            flops=3_400_000_000, bytes_accessed=4 << 20, transcendentals=0
        ),
        name="fused",
    )(
        nrm[0],
        jnp.swapaxes(w1[0], 0, 1),
        jnp.swapaxes(w2[0], 0, 1),
        wout[0],
        pext[0].reshape(ROWS, NX, NQ, ROWS, PC),
        gain,
    )
    return out[None]


def solution(mesh):
    in_specs = (
        P("section", "res", None, None),
        P("section", None, None),
        P("section", None, None),
        P("section", None, None),
        P("section", "res", None, None),
        P("section", None),
    )
    out_specs = P("section", "res", None, None)
    return jax.shard_map(shards, mesh=mesh, in_specs=in_specs, out_specs=out_specs, check_vma=False)
```

```python
import jax
import jax.numpy as jnp
from jax import lax
from jax.experimental import pallas as pl
from jax.experimental.pallas import tpu as pltpu
from jax.sharding import PartitionSpec as P

MESH = pl.DeviceIdType.MESH
BF = jnp.bfloat16
F32 = jnp.float32
NSEC = 16
NRES = 16
ROWS = 16
SEQ = 128
CH = 256
W = 32
PC = 128
NX, NZ, NC = 4, 2, 2
NQ = NZ * NC
JC = NX * ROWS
YP = W // 2
YG = 4
YN = W // YG
STEP = 8


def kernel(
    nrm_hbm, w1_hbm, w2_hbm, wout_hbm, pext_hbm, gain_hbm, lr_hbm,
    nrm, w1, w2, wout, gain, gsend, gall,
    fr, bs, ph, wf, wp, lf, lt, rf, rall, osc, lacc, rg, c1, xs, xr, zs, zr, rgf, wt, lrv,
    in_sem, gs_sem, gr_sem, fs_sem, fr_sem, bs_sem, br_sem, as_sem, ar_sem,
    cs_sem, cr_sem, xs_sem, xr_sem, zs_sem, zr_sem, out_sem,
):
    sec = lax.axis_index("section")
    res = lax.axis_index("res")
    mx, mz, mc = res // 4, lax.rem(res // 2, 2), lax.rem(res, 2)

    def at(x, z, c):
        return (sec, x * 4 + z * 2 + c)

    other_core = at(mx, mz, 1 - mc)
    other_z = at(mx, 1 - mz, mc)

    def x_peer(d):
        x = lax.rem(mx + d, NX)
        return x, at(x, mz, mc)

    loads = [
        pltpu.make_async_copy(src, dst, in_sem.at[n])
        for n, (src, dst) in enumerate(
            [(gain_hbm, gain), (nrm_hbm, nrm), (w1_hbm, w1), (w2_hbm, w2), (wout_hbm, wout)]
        )
    ]
    for load in loads:
        load.start()

    barrier = pltpu.get_barrier_semaphore()

    def greet(d, _):
        pl.semaphore_signal(
            barrier, inc=1, device_id=(lax.rem(sec + d, NSEC), res), device_id_type=MESH
        )
        return 0

    lax.fori_loop(1, NSEC, greet, 0)
    pl.semaphore_signal(barrier, inc=1, device_id=other_core, device_id_type=MESH)
    pl.semaphore_signal(barrier, inc=1, device_id=other_z, device_id_type=MESH)
    for d in range(1, NX):
        pl.semaphore_signal(barrier, inc=1, device_id=x_peer(d)[1], device_id_type=MESH)
    loads[0].wait()
    gsend[...] = jnp.broadcast_to(gain[...], gsend.shape)
    gall[sec] = gsend[...]
    pl.semaphore_wait(barrier, NSEC - 1 + 2 + NX - 1)

    def fwd(c, d):
        peer = lax.rem(sec + d, NSEC)
        return pltpu.make_async_remote_copy(
            src_ref=pext_hbm.at[peer, :, c],
            dst_ref=fr.at[c, sec],
            send_sem=fs_sem.at[c, d],
            recv_sem=fr_sem.at[c, sec],
            device_id=(peer, res),
            device_id_type=MESH,
        )

    def gains(d):
        peer = lax.rem(sec + d, NSEC)
        return pltpu.make_async_remote_copy(
            src_ref=gsend,
            dst_ref=gall.at[sec],
            send_sem=gs_sem.at[d],
            recv_sem=gr_sem.at[sec],
            device_id=(peer, res),
            device_id_type=MESH,
        )

    def each(body, low=1, high=NSEC):
        def step(d, _):
            body(d)
            return 0

        lax.fori_loop(low, high, step, 0)

    def send_fwd(c):
        each(lambda d: fwd(c, d).start())
        pltpu.make_async_copy(pext_hbm.at[sec, :, c], fr.at[c, sec], fr_sem.at[c, sec]).start()

    send_fwd(0)
    each(lambda d: gains(d).start())
    send_fwd(1)

    loads[1].wait()
    loads[2].wait()
    loads[3].wait()
    wt[:W] = w1[...]
    wt[W:] = w2[...]

    def project(n, _):
        block = nrm[pl.ds(n * 2, 2)].reshape(2 * SEQ, CH)
        both = lax.dot_general(
            wt[...], block, (((1,), (1,)), ((), ())), preferred_element_type=F32
        )
        for t in range(2):
            rows = pl.multiple_of((n * 2 + t) * W, W)
            lf[pl.ds(rows, W), :] = both[:W, t * SEQ : (t + 1) * SEQ]
            rf[pl.ds(rows, W), :] = both[W:, t * SEQ : (t + 1) * SEQ]
        return 0

    lax.fori_loop(0, ROWS // 2, project, 0)
    for y in range(W):
        rall[mx, mz, mc, y] = rf[pl.ds(y, ROWS, stride=W), :].astype(BF)

    def share(n, x, z, c, to):
        return pltpu.make_async_remote_copy(
            src_ref=rall.at[x, z, c],
            dst_ref=rall.at[x, z, c],
            send_sem=as_sem.at[n],
            recv_sem=ar_sem.at[x, z, c],
            device_id=to,
            device_id_type=MESH,
        )

    def arrived(x, z, c):
        pltpu.make_async_copy(rall.at[x, z, c], rall.at[x, z, c], ar_sem.at[x, z, c]).wait()

    shares = []

    def pass_on(copies):
        for copy in copies:
            copy.start()
        shares.extend(copies)

    pass_on(
        [share(0, mx, mz, mc, other_z)]
        + [share(d, mx, mz, mc, x_peer(d)[1]) for d in range(1, NX)]
        + [share(4, mx, mz, mc, other_core)]
    )
    send_fwd(2)
    send_fwd(3)

    for n in range(4):
        lt[:, n * 128 : (n + 1) * 128] = lf[n * 128 : (n + 1) * 128, :].T.astype(BF)
    loads[4].wait()
    wf[...] = wout[...].astype(F32)
    for y in range(W):
        wp[(y // 2) * W : (y // 2 + 1) * W, (y % 2) * PC : (y % 2 + 1) * PC] = wf[
            pl.ds(y, W, stride=W), :
        ].astype(BF)
    lacc[...] = jnp.zeros_like(lacc)

    def pass_z():
        arrived(mx, 1 - mz, mc)
        pass_on(
            [share(4 + d, mx, 1 - mz, mc, x_peer(d)[1]) for d in range(1, NX)]
            + [share(8, mx, 1 - mz, mc, other_core)]
        )

    def pass_x(n):
        for d in range(1, NX):
            x = x_peer(d)[0]
            z = mz if n == 0 else 1 - mz
            arrived(x, z, mc)
            pass_on([share(7 + 2 * d + n, x, z, mc, other_core)])

    def back(c, d):
        peer = lax.rem(sec + d, NSEC)
        return pltpu.make_async_remote_copy(
            src_ref=bs.at[c, peer],
            dst_ref=ph.at[c, sec],
            send_sem=bs_sem.at[c, d],
            recv_sem=br_sem.at[c, sec],
            device_id=(peer, res),
            device_id_type=MESH,
        )

    def gain_arrived(d):
        k = lax.rem(sec + d, NSEC)
        pltpu.make_async_copy(gall.at[k], gall.at[k], gr_sem.at[k]).wait()

    def scan(c):
        if c == 0:
            each(gain_arrived)
        each(lambda k: pltpu.make_async_copy(fr.at[c, k], fr.at[c, k], fr_sem.at[c, k]).wait(), 0)
        total = None
        for k in range(NSEC - 1, -1, -1):
            grad = fr[c, k].reshape(JC, PC).astype(F32)
            total = grad if total is None else grad + gall[k + 1, 0:1, :] * total
            bs[c, k] = total.astype(BF).reshape(NX, ROWS, PC)
        pltpu.make_async_copy(bs.at[c, sec], ph.at[c, sec], br_sem.at[c, sec]).start()
        each(lambda d: back(c, d).start())

    def core_copy(c, g):
        ys = pl.ds(g * YN, YN)
        return pltpu.make_async_remote_copy(
            src_ref=rg.at[c, :, ys],
            dst_ref=c1.at[c // 2, :, ys],
            send_sem=cs_sem.at[c, g],
            recv_sem=cr_sem.at[c // 2, g],
            device_id=other_core,
            device_id_type=MESH,
        )

    def x_copy(c, g, d):
        ys = pl.ds(g * YN, YN)
        x, peer = x_peer(d)
        return pltpu.make_async_remote_copy(
            src_ref=xs.at[c // 2, x, ys],
            dst_ref=xr.at[c // 2, mx, ys],
            send_sem=xs_sem.at[c // 2, g, d],
            recv_sem=xr_sem.at[c // 2, g, mx],
            device_id=peer,
            device_id_type=MESH,
        )

    def z_copy(g):
        ys = pl.ds(g * YN, YN)
        return pltpu.make_async_remote_copy(
            src_ref=zs.at[1 - mz, ys],
            dst_ref=zr.at[ys],
            send_sem=zs_sem.at[g],
            recv_sem=zr_sem.at[g],
            device_id=other_z,
            device_id_type=MESH,
        )

    def products(c):
        def outer(n, _):
            rows = [lax.rem(sec - n * 4 - t + NSEC, NSEC) for t in range(4)]
            for i in rows:
                pltpu.make_async_copy(ph.at[c, i], ph.at[c, i], br_sem.at[c, i]).wait()
            for two in (rows[:2], rows[2:]):
                wide = []
                for i in two:
                    pair = ph[c, i].reshape(JC, PC)
                    none = jnp.zeros_like(pair)
                    wide += [
                        jnp.concatenate([pair, none], axis=1),
                        jnp.concatenate([none, pair], axis=1),
                    ]
                grad = lax.dot_general(
                    wp[...],
                    jnp.concatenate(wide, axis=0),
                    (((1,), (1,)), ((), ())),
                    preferred_element_type=F32,
                ).astype(BF)
                for t, i in enumerate(two):
                    osc[c, i] = grad[:, t * 2 * JC : (t + 1) * 2 * JC].reshape(YP, W, 2 * JC)
            return 0

        lax.fori_loop(0, ROWS // 4, outer, 0)

        for g in range(YG):

            def right(n, _):
                for h in range(2):
                    yp = g * (YN // 2) + n * 4 + h * 2
                    both = jnp.concatenate(
                        [osc[c, :, yp + t].reshape(ROWS * W, 2 * JC) for t in range(2)], axis=1
                    )
                    grad = jnp.dot(lt[...], both, preferred_element_type=F32)
                    for t in range(2):
                        turned = grad[:, t * 2 * JC : (t + 1) * 2 * JC].T.astype(BF)
                        turned = turned.reshape(2, NX, ROWS, SEQ)
                        for u in range(2):
                            rg[c, :, (yp + t) * 2 + u] = turned[u]
                return 0

            lax.fori_loop(0, YN // 8, right, 0)

            @pl.when(mc != c % 2)
            def _():
                core_copy(c, g).start()

    def left_products(c):
        def left(n, _):
            terms = jnp.concatenate(
                [osc[c, :, n * 8 + t].reshape(ROWS * W, 2 * JC) for t in range(8)], axis=1
            )
            vectors = jnp.concatenate(
                [rall[:, c // 2, c % 2, n * 16 + t].reshape(JC, SEQ) for t in range(16)], axis=0
            )
            lacc[...] += jnp.dot(terms, vectors, preferred_element_type=F32)
            return 0

        lax.fori_loop(0, YP // 8, left, 0)

    def over_cores(c):
        @pl.when(mc == c % 2)
        def _():
            for g in range(YG):
                core_copy(c, g).wait_recv()

                def add_core(n, _):
                    y = g * YN + n
                    xs[c // 2, :, y] = (
                        rg[c, :, y].astype(F32) + c1[c // 2, :, y].astype(F32)
                    ).astype(BF)
                    return 0

                lax.fori_loop(0, YN, add_core, 0)
                for d in range(1, NX):
                    x_copy(c, g, d).start()

    def over_x(c):
        @pl.when(mc == c % 2)
        def _():
            for g in range(YG):
                for d in range(1, NX):
                    x = x_peer(d)[0]
                    part = xr.at[c // 2, x, pl.ds(g * YN, YN)]
                    pltpu.make_async_copy(part, part, xr_sem.at[c // 2, g, x]).wait()

                def add_x(n, _):
                    y = g * YN + n
                    total = xs[c // 2, mx, y].astype(F32)
                    for d in range(1, NX):
                        total += xr[c // 2, x_peer(d)[0], y].astype(F32)
                    zs[c // 2, y] = total.astype(BF)
                    return 0

                lax.fori_loop(0, YN, add_x, 0)

                @pl.when(mz != c // 2)
                def _():
                    z_copy(g).start()

    def over_z():
        for g in range(YG):
            z_copy(g).wait_recv()

            def add_z(n, _):
                y = g * YN + n
                rows = pl.multiple_of(y * ROWS, ROWS)
                rgf[pl.ds(rows, ROWS), :] = zs[mz, y].astype(F32) + zr[y].astype(F32)
                return 0

            lax.fori_loop(0, YN, add_z, 0)

    scan(0)
    pass_z()
    scan(1)
    scan(2)
    pass_x(0)
    scan(3)
    pass_x(1)
    for c in range(NQ):
        products(c)
        if c == 1:
            for x in range(NX):
                for z in range(NZ):
                    arrived(x, z, 1 - mc)
        if c:
            left_products(c - 1)
            over_x(c - 1)
        over_cores(c)
    left_products(NQ - 1)
    for i in range(ROWS):
        lrv[i, :W] = (lacc[i * W : (i + 1) * W, :] * (1.0 / SEQ)).astype(BF)
    over_x(NQ - 1)
    over_z()

    for i in range(ROWS):
        lrv[i, W:] = (rgf[pl.ds(i, W, stride=ROWS), :] * (1.0 / SEQ)).astype(BF)
    done = pltpu.make_async_copy(lrv, lr_hbm, out_sem)
    done.start()

    for c in range(NQ):
        each(lambda d: fwd(c, d).wait_send())
        each(lambda d: back(c, d).wait_send())
    each(lambda d: gains(d).wait_send())
    for copy in shares:
        copy.wait_send()
    for c in range(NQ):
        for g in range(YG):

            @pl.when(mc != c % 2)
            def _():
                core_copy(c, g).wait_send()

            @pl.when(mc == c % 2)
            def _():
                for d in range(1, NX):
                    x_copy(c, g, d).wait_send()

    for g in range(YG):
        z_copy(g).wait_send()
    done.wait()


def project_out(lr, w1, w2, out):
    weights = jnp.concatenate([w1[...], w2[...]], axis=0)
    for t in range(STEP):
        out[t] = lax.dot_general(
            lr[t], weights, (((0,), (0,)), ((), ())), preferred_element_type=F32
        ).astype(BF)


def shards(nrm, w1, w2, wout, pext, gain):
    anyspace = pl.BlockSpec(memory_space=pl.ANY)
    vm = pltpu.VMEM
    dma = pltpu.SemaphoreType.DMA
    w1t = jnp.swapaxes(w1[0], 0, 1)
    w2t = jnp.swapaxes(w2[0], 0, 1)
    lr = pl.pallas_call(
        kernel,
        out_shape=jax.ShapeDtypeStruct((ROWS, 2 * W, SEQ), BF),
        in_specs=[anyspace] * 6,
        out_specs=anyspace,
        scratch_shapes=[
            vm((ROWS, SEQ, CH), BF),
            vm((W, CH), BF),
            vm((W, CH), BF),
            vm((W * W, PC), BF),
            vm((1, PC), F32),
            vm((8, PC), F32),
            vm((NSEC, 8, PC), F32),
            vm((NQ, NSEC, NX, ROWS, PC), BF),
            vm((NQ, NSEC, NX, ROWS, PC), BF),
            vm((NQ, NSEC, NX, ROWS, PC), BF),
            vm((W * W, PC), F32),
            vm((YP * W, 2 * PC), BF),
            vm((ROWS * W, SEQ), F32),
            vm((SEQ, ROWS * W), BF),
            vm((ROWS * W, SEQ), F32),
            vm((NX, NZ, NC, W, ROWS, SEQ), BF),
            vm((NQ, ROWS, YP, W, 2 * JC), BF),
            vm((ROWS * W, SEQ), F32),
            vm((NQ, NX, W, ROWS, SEQ), BF),
            vm((2, NX, W, ROWS, SEQ), BF),
            vm((2, NX, W, ROWS, SEQ), BF),
            vm((2, NX, W, ROWS, SEQ), BF),
            vm((2, W, ROWS, SEQ), BF),
            vm((W, ROWS, SEQ), BF),
            vm((W * ROWS, SEQ), F32),
            vm((2 * W, CH), BF),
            vm((ROWS, 2 * W, SEQ), BF),
            dma((5,)),
            dma((NSEC,)),
            dma((NSEC,)),
            dma((NQ, NSEC)),
            dma((NQ, NSEC)),
            dma((NQ, NSEC)),
            dma((NQ, NSEC)),
            dma((16,)),
            dma((NX, NZ, NC)),
            dma((NQ, YG)),
            dma((NZ, YG)),
            dma((NZ, YG, NX)),
            dma((NZ, YG, NX)),
            dma((YG,)),
            dma((YG,)),
            dma,
        ],
        compiler_params=pltpu.CompilerParams(
            collective_id=0, has_side_effects=True, vmem_limit_bytes=56 << 20
        ),
        cost_estimate=pl.CostEstimate(
            flops=3_400_000_000, bytes_accessed=4 << 20, transcendentals=0
        ),
        name="fused",
    )(
        nrm[0],
        w1t,
        w2t,
        wout[0],
        pext[0].reshape(ROWS, NX, NQ, ROWS, PC),
        gain,
    )
    out = pl.pallas_call(
        project_out,
        out_shape=jax.ShapeDtypeStruct((ROWS, SEQ, CH), BF),
        grid=(ROWS // STEP,),
        in_specs=[
            pl.BlockSpec((STEP, 2 * W, SEQ), lambda n: (n, 0, 0)),
            pl.BlockSpec((W, CH), lambda n: (0, 0)),
            pl.BlockSpec((W, CH), lambda n: (0, 0)),
        ],
        out_specs=pl.BlockSpec((STEP, SEQ, CH), lambda n: (n, 0, 0)),
        name="project_out",
    )(lr, w1t, w2t)
    return out[None]


def solution(mesh):
    in_specs = (
        P("section", "res", None, None),
        P("section", None, None),
        P("section", None, None),
        P("section", None, None),
        P("section", "res", None, None),
        P("section", None),
    )
    out_specs = P("section", "res", None, None)
    return jax.shard_map(shards, mesh=mesh, in_specs=in_specs, out_specs=out_specs, check_vma=False)
```

```python
import jax
import jax.numpy as jnp
from jax import lax
from jax.experimental import pallas as pl
from jax.experimental.pallas import tpu as pltpu
from jax.sharding import PartitionSpec as P

MESH = pl.DeviceIdType.MESH
BF = jnp.bfloat16
F32 = jnp.float32
NSEC = 16
NRES = 16
ROWS = 16
SEQ = 128
CH = 256
W = 32
PC = 128
NX, NZ, NC = 4, 2, 2
NQ = NZ * NC
JC = NX * ROWS
YP = W // 2
YG = 4
YN = W // YG
STEP = 8


def kernel(
    nrm_hbm, w1_hbm, w2_hbm, wout_hbm, pext_hbm, gain_hbm, lr_hbm,
    nrm, w1, w2, wout, gain, gsend, gall,
    fr, bs, ph, wf, wp, lf, lt, rf, rall, osc, lacc, rg, c1, xs, xr, zs, zr, rgf, wt, lrv,
    in_sem, gs_sem, gr_sem, fs_sem, fr_sem, bs_sem, br_sem, as_sem, ar_sem,
    cs_sem, cr_sem, xs_sem, xr_sem, zs_sem, zr_sem, out_sem,
):
    sec = lax.axis_index("section")
    res = lax.axis_index("res")
    mx, mz, mc = res // 4, lax.rem(res // 2, 2), lax.rem(res, 2)

    def at(x, z, c):
        return (sec, x * 4 + z * 2 + c)

    other_core = at(mx, mz, 1 - mc)
    other_z = at(mx, 1 - mz, mc)

    def x_peer(d):
        x = lax.rem(mx + d, NX)
        return x, at(x, mz, mc)

    loads = [
        pltpu.make_async_copy(src, dst, in_sem.at[n])
        for n, (src, dst) in enumerate(
            [(gain_hbm, gain), (nrm_hbm, nrm), (w1_hbm, w1), (w2_hbm, w2), (wout_hbm, wout)]
        )
    ]
    for load in loads:
        load.start()

    barrier = pltpu.get_barrier_semaphore()

    def greet(d, _):
        pl.semaphore_signal(
            barrier, inc=1, device_id=(lax.rem(sec + d, NSEC), res), device_id_type=MESH
        )
        return 0

    lax.fori_loop(1, NSEC, greet, 0)
    pl.semaphore_signal(barrier, inc=1, device_id=other_core, device_id_type=MESH)
    pl.semaphore_signal(barrier, inc=1, device_id=other_z, device_id_type=MESH)
    for d in range(1, NX):
        pl.semaphore_signal(barrier, inc=1, device_id=x_peer(d)[1], device_id_type=MESH)
    loads[0].wait()
    gsend[...] = jnp.broadcast_to(gain[...], gsend.shape)
    gall[sec] = gsend[...]
    pl.semaphore_wait(barrier, NSEC - 1 + 2 + NX - 1)

    def fwd(c, d):
        peer = lax.rem(sec + d, NSEC)
        return pltpu.make_async_remote_copy(
            src_ref=pext_hbm.at[peer, :, c],
            dst_ref=fr.at[c, sec],
            send_sem=fs_sem.at[c, d],
            recv_sem=fr_sem.at[c, sec],
            device_id=(peer, res),
            device_id_type=MESH,
        )

    def gains(d):
        peer = lax.rem(sec + d, NSEC)
        return pltpu.make_async_remote_copy(
            src_ref=gsend,
            dst_ref=gall.at[sec],
            send_sem=gs_sem.at[d],
            recv_sem=gr_sem.at[sec],
            device_id=(peer, res),
            device_id_type=MESH,
        )

    def each(body, low=1, high=NSEC):
        def step(d, _):
            body(d)
            return 0

        lax.fori_loop(low, high, step, 0)

    def send_fwd(c):
        each(lambda d: fwd(c, d).start())
        pltpu.make_async_copy(pext_hbm.at[sec, :, c], fr.at[c, sec], fr_sem.at[c, sec]).start()

    send_fwd(0)
    each(lambda d: gains(d).start())
    send_fwd(1)
    send_fwd(2)
    send_fwd(3)

    loads[1].wait()
    loads[2].wait()
    loads[3].wait()
    wt[:W] = w1[...]
    wt[W:] = w2[...]

    def project(n, _):
        block = nrm[pl.ds(n * 2, 2)].reshape(2 * SEQ, CH)
        both = lax.dot_general(
            wt[...], block, (((1,), (1,)), ((), ())), preferred_element_type=F32
        )
        for t in range(2):
            rows = pl.multiple_of((n * 2 + t) * W, W)
            lf[pl.ds(rows, W), :] = both[:W, t * SEQ : (t + 1) * SEQ]
            rf[pl.ds(rows, W), :] = both[W:, t * SEQ : (t + 1) * SEQ]
        return 0

    lax.fori_loop(0, ROWS // 2, project, 0)
    for y in range(W):
        rall[mx, mz, mc, y] = rf[pl.ds(y, ROWS, stride=W), :].astype(BF)

    def share(n, x, z, c, to):
        return pltpu.make_async_remote_copy(
            src_ref=rall.at[x, z, c],
            dst_ref=rall.at[x, z, c],
            send_sem=as_sem.at[n],
            recv_sem=ar_sem.at[x, z, c],
            device_id=to,
            device_id_type=MESH,
        )

    def arrived(x, z, c):
        pltpu.make_async_copy(rall.at[x, z, c], rall.at[x, z, c], ar_sem.at[x, z, c]).wait()

    shares = []

    def pass_on(copies):
        for copy in copies:
            copy.start()
        shares.extend(copies)

    pass_on(
        [share(0, mx, mz, mc, other_z)]
        + [share(d, mx, mz, mc, x_peer(d)[1]) for d in range(1, NX)]
        + [share(4, mx, mz, mc, other_core)]
    )

    for n in range(4):
        lt[:, n * 128 : (n + 1) * 128] = lf[n * 128 : (n + 1) * 128, :].T.astype(BF)
    loads[4].wait()
    wf[...] = wout[...].astype(F32)
    for y in range(W):
        wp[(y // 2) * W : (y // 2 + 1) * W, (y % 2) * PC : (y % 2 + 1) * PC] = wf[
            pl.ds(y, W, stride=W), :
        ].astype(BF)
    lacc[...] = jnp.zeros_like(lacc)

    def pass_z():
        arrived(mx, 1 - mz, mc)
        pass_on(
            [share(4 + d, mx, 1 - mz, mc, x_peer(d)[1]) for d in range(1, NX)]
            + [share(8, mx, 1 - mz, mc, other_core)]
        )

    def pass_x(n):
        for d in range(1, NX):
            x = x_peer(d)[0]
            z = mz if n == 0 else 1 - mz
            arrived(x, z, mc)
            pass_on([share(7 + 2 * d + n, x, z, mc, other_core)])

    def back(c, d):
        peer = lax.rem(sec + d, NSEC)
        return pltpu.make_async_remote_copy(
            src_ref=bs.at[c, peer],
            dst_ref=ph.at[c, sec],
            send_sem=bs_sem.at[c, d],
            recv_sem=br_sem.at[c, sec],
            device_id=(peer, res),
            device_id_type=MESH,
        )

    def gain_arrived(d):
        k = lax.rem(sec + d, NSEC)
        pltpu.make_async_copy(gall.at[k], gall.at[k], gr_sem.at[k]).wait()

    def scan(c):
        if c == 0:
            each(gain_arrived)
        each(lambda k: pltpu.make_async_copy(fr.at[c, k], fr.at[c, k], fr_sem.at[c, k]).wait(), 0)
        total = None
        for k in range(NSEC - 1, -1, -1):
            grad = fr[c, k].reshape(JC, PC).astype(F32)
            total = grad if total is None else grad + gall[k + 1, 0:1, :] * total
            bs[c, k] = total.astype(BF).reshape(NX, ROWS, PC)
        pltpu.make_async_copy(bs.at[c, sec], ph.at[c, sec], br_sem.at[c, sec]).start()
        each(lambda d: back(c, d).start())

    def core_copy(c, g):
        ys = pl.ds(g * YN, YN)
        return pltpu.make_async_remote_copy(
            src_ref=rg.at[c, :, ys],
            dst_ref=c1.at[c // 2, :, ys],
            send_sem=cs_sem.at[c, g],
            recv_sem=cr_sem.at[c // 2, g],
            device_id=other_core,
            device_id_type=MESH,
        )

    def x_copy(c, g, d):
        ys = pl.ds(g * YN, YN)
        x, peer = x_peer(d)
        return pltpu.make_async_remote_copy(
            src_ref=xs.at[c // 2, x, ys],
            dst_ref=xr.at[c // 2, mx, ys],
            send_sem=xs_sem.at[c // 2, g, d],
            recv_sem=xr_sem.at[c // 2, g, mx],
            device_id=peer,
            device_id_type=MESH,
        )

    def z_copy(g):
        ys = pl.ds(g * YN, YN)
        return pltpu.make_async_remote_copy(
            src_ref=zs.at[1 - mz, ys],
            dst_ref=zr.at[ys],
            send_sem=zs_sem.at[g],
            recv_sem=zr_sem.at[g],
            device_id=other_z,
            device_id_type=MESH,
        )

    def products(c):
        def outer(n, _):
            rows = [lax.rem(sec - n * 4 - t + NSEC, NSEC) for t in range(4)]
            for i in rows:
                pltpu.make_async_copy(ph.at[c, i], ph.at[c, i], br_sem.at[c, i]).wait()
            for two in (rows[:2], rows[2:]):
                wide = []
                for i in two:
                    pair = ph[c, i].reshape(JC, PC)
                    none = jnp.zeros_like(pair)
                    wide += [
                        jnp.concatenate([pair, none], axis=1),
                        jnp.concatenate([none, pair], axis=1),
                    ]
                grad = lax.dot_general(
                    wp[...],
                    jnp.concatenate(wide, axis=0),
                    (((1,), (1,)), ((), ())),
                    preferred_element_type=F32,
                ).astype(BF)
                for t, i in enumerate(two):
                    osc[c, i] = grad[:, t * 2 * JC : (t + 1) * 2 * JC].reshape(YP, W, 2 * JC)
            return 0

        lax.fori_loop(0, ROWS // 4, outer, 0)

        for g in range(YG):

            def right(n, _):
                for h in range(2):
                    yp = g * (YN // 2) + n * 4 + h * 2
                    both = jnp.concatenate(
                        [osc[c, :, yp + t].reshape(ROWS * W, 2 * JC) for t in range(2)], axis=1
                    )
                    grad = jnp.dot(lt[...], both, preferred_element_type=F32)
                    for t in range(2):
                        turned = grad[:, t * 2 * JC : (t + 1) * 2 * JC].T.astype(BF)
                        turned = turned.reshape(2, NX, ROWS, SEQ)
                        for u in range(2):
                            rg[c, :, (yp + t) * 2 + u] = turned[u]
                return 0

            lax.fori_loop(0, YN // 8, right, 0)

            @pl.when(mc != c % 2)
            def _():
                core_copy(c, g).start()

    def left_products(c):
        def left(n, _):
            terms = jnp.concatenate(
                [osc[c, :, n * 8 + t].reshape(ROWS * W, 2 * JC) for t in range(8)], axis=1
            )
            vectors = jnp.concatenate(
                [rall[:, c // 2, c % 2, n * 16 + t].reshape(JC, SEQ) for t in range(16)], axis=0
            )
            lacc[...] += jnp.dot(terms, vectors, preferred_element_type=F32)
            return 0

        lax.fori_loop(0, YP // 8, left, 0)

    def over_cores(c):
        @pl.when(mc == c % 2)
        def _():
            for g in range(YG):
                core_copy(c, g).wait_recv()

                def add_core(n, _):
                    y = g * YN + n
                    xs[c // 2, :, y] = (
                        rg[c, :, y].astype(F32) + c1[c // 2, :, y].astype(F32)
                    ).astype(BF)
                    return 0

                lax.fori_loop(0, YN, add_core, 0)
                for d in range(1, NX):
                    x_copy(c, g, d).start()

    def over_x(c):
        @pl.when(mc == c % 2)
        def _():
            for g in range(YG):
                for d in range(1, NX):
                    x = x_peer(d)[0]
                    part = xr.at[c // 2, x, pl.ds(g * YN, YN)]
                    pltpu.make_async_copy(part, part, xr_sem.at[c // 2, g, x]).wait()

                def add_x(n, _):
                    y = g * YN + n
                    total = xs[c // 2, mx, y].astype(F32)
                    for d in range(1, NX):
                        total += xr[c // 2, x_peer(d)[0], y].astype(F32)
                    zs[c // 2, y] = total.astype(BF)
                    return 0

                lax.fori_loop(0, YN, add_x, 0)

                @pl.when(mz != c // 2)
                def _():
                    z_copy(g).start()

    def over_z():
        for g in range(YG):
            z_copy(g).wait_recv()

            def add_z(n, _):
                y = g * YN + n
                rows = pl.multiple_of(y * ROWS, ROWS)
                rgf[pl.ds(rows, ROWS), :] = zs[mz, y].astype(F32) + zr[y].astype(F32)
                return 0

            lax.fori_loop(0, YN, add_z, 0)

    def sent_fwd():
        for c in range(NQ):
            each(lambda d: fwd(c, d).wait_send())
        each(lambda d: gains(d).wait_send())

    def sent_back():
        for c in range(NQ):
            each(lambda d: back(c, d).wait_send())
        for copy in shares:
            copy.wait_send()

    def sent(c):
        @pl.when(mc != c % 2)
        def _():
            for g in range(YG):
                core_copy(c, g).wait_send()

        @pl.when(mc == c % 2)
        def _():
            for g in range(YG):
                for d in range(1, NX):
                    x_copy(c, g, d).wait_send()

    def sent_z():
        for g in range(YG):
            z_copy(g).wait_send()

    scan(0)
    scan(1)
    scan(2)
    scan(3)
    pass_z()
    pass_x(0)
    products(0)
    over_cores(0)
    pass_x(1)
    products(1)
    over_x(0)
    over_cores(1)
    products(2)
    for x in range(NX):
        for z in range(NZ):
            arrived(x, z, 1 - mc)
    left_products(0)
    left_products(1)
    over_x(1)
    over_cores(2)
    sent_fwd()
    products(3)
    over_x(2)
    over_cores(3)
    left_products(2)
    left_products(3)
    for i in range(ROWS):
        lrv[i, :W] = (lacc[i * W : (i + 1) * W, :] * (1.0 / SEQ)).astype(BF)
    sent(0)
    sent(1)
    sent(2)
    sent_back()
    over_x(NQ - 1)
    over_z()

    for i in range(ROWS):
        lrv[i, W:] = (rgf[pl.ds(i, W, stride=ROWS), :] * (1.0 / SEQ)).astype(BF)
    done = pltpu.make_async_copy(lrv, lr_hbm, out_sem)
    done.start()
    sent(3)
    sent_z()

    done.wait()


def project_out(lr, w1, w2, out):
    weights = jnp.concatenate([w1[...], w2[...]], axis=0)
    for t in range(STEP):
        out[t] = lax.dot_general(
            lr[t], weights, (((0,), (0,)), ((), ())), preferred_element_type=F32
        ).astype(BF)


def shards(nrm, w1, w2, wout, pext, gain):
    anyspace = pl.BlockSpec(memory_space=pl.ANY)
    vm = pltpu.VMEM
    dma = pltpu.SemaphoreType.DMA
    w1t = jnp.swapaxes(w1[0], 0, 1)
    w2t = jnp.swapaxes(w2[0], 0, 1)
    lr = pl.pallas_call(
        kernel,
        out_shape=jax.ShapeDtypeStruct((ROWS, 2 * W, SEQ), BF),
        in_specs=[anyspace] * 6,
        out_specs=anyspace,
        scratch_shapes=[
            vm((ROWS, SEQ, CH), BF),
            vm((W, CH), BF),
            vm((W, CH), BF),
            vm((W * W, PC), BF),
            vm((1, PC), F32),
            vm((8, PC), F32),
            vm((NSEC, 8, PC), F32),
            vm((NQ, NSEC, NX, ROWS, PC), BF),
            vm((NQ, NSEC, NX, ROWS, PC), BF),
            vm((NQ, NSEC, NX, ROWS, PC), BF),
            vm((W * W, PC), F32),
            vm((YP * W, 2 * PC), BF),
            vm((ROWS * W, SEQ), F32),
            vm((SEQ, ROWS * W), BF),
            vm((ROWS * W, SEQ), F32),
            vm((NX, NZ, NC, W, ROWS, SEQ), BF),
            vm((NQ, ROWS, YP, W, 2 * JC), BF),
            vm((ROWS * W, SEQ), F32),
            vm((NQ, NX, W, ROWS, SEQ), BF),
            vm((2, NX, W, ROWS, SEQ), BF),
            vm((2, NX, W, ROWS, SEQ), BF),
            vm((2, NX, W, ROWS, SEQ), BF),
            vm((2, W, ROWS, SEQ), BF),
            vm((W, ROWS, SEQ), BF),
            vm((W * ROWS, SEQ), F32),
            vm((2 * W, CH), BF),
            vm((ROWS, 2 * W, SEQ), BF),
            dma((5,)),
            dma((NSEC,)),
            dma((NSEC,)),
            dma((NQ, NSEC)),
            dma((NQ, NSEC)),
            dma((NQ, NSEC)),
            dma((NQ, NSEC)),
            dma((16,)),
            dma((NX, NZ, NC)),
            dma((NQ, YG)),
            dma((NZ, YG)),
            dma((NZ, YG, NX)),
            dma((NZ, YG, NX)),
            dma((YG,)),
            dma((YG,)),
            dma,
        ],
        compiler_params=pltpu.CompilerParams(
            collective_id=0, has_side_effects=True, vmem_limit_bytes=56 << 20
        ),
        cost_estimate=pl.CostEstimate(
            flops=3_400_000_000, bytes_accessed=4 << 20, transcendentals=0
        ),
        name="fused",
    )(
        nrm[0],
        w1t,
        w2t,
        wout[0],
        pext[0].reshape(ROWS, NX, NQ, ROWS, PC),
        gain,
    )
    out = pl.pallas_call(
        project_out,
        out_shape=jax.ShapeDtypeStruct((ROWS, SEQ, CH), BF),
        grid=(ROWS // STEP,),
        in_specs=[
            pl.BlockSpec((STEP, 2 * W, SEQ), lambda n: (n, 0, 0)),
            pl.BlockSpec((W, CH), lambda n: (0, 0)),
            pl.BlockSpec((W, CH), lambda n: (0, 0)),
        ],
        out_specs=pl.BlockSpec((STEP, SEQ, CH), lambda n: (n, 0, 0)),
        name="project_out",
    )(lr, w1t, w2t)
    return out[None]


def solution(mesh):
    in_specs = (
        P("section", "res", None, None),
        P("section", None, None),
        P("section", None, None),
        P("section", None, None),
        P("section", "res", None, None),
        P("section", None),
    )
    out_specs = P("section", "res", None, None)
    return jax.shard_map(shards, mesh=mesh, in_specs=in_specs, out_specs=out_specs, check_vma=False)
```

```python
import jax
import jax.numpy as jnp
from jax import lax
from jax.experimental import pallas as pl
from jax.experimental.pallas import tpu as pltpu
from jax.sharding import PartitionSpec as P

MESH = pl.DeviceIdType.MESH
BF = jnp.bfloat16
F32 = jnp.float32
NSEC = 16
NRES = 16
ROWS = 16
SEQ = 128
CH = 256
W = 32
PC = 128
NX, NZ, NC = 4, 2, 2
NQ = NZ * NC
JC = NX * ROWS
YP = W // 2
YG = 4
YN = W // YG
STEP = 8


def kernel(
    nrm_hbm, w1_hbm, w2_hbm, wout_hbm, pext_hbm, gain_hbm, lr_hbm,
    nrm, w1, w2, wout, gain, gsend, gall,
    fr, bs, ph, wf, wp, lf, lt, rf, rall, osc, lacc, rg, c1, xs, xr, zs, zr, rgf, wt, lrv,
    in_sem, gs_sem, gr_sem, fs_sem, fr_sem, bs_sem, br_sem, as_sem, ar_sem,
    cs_sem, cr_sem, xs_sem, xr_sem, zs_sem, zr_sem, out_sem,
):
    sec = lax.axis_index("section")
    res = lax.axis_index("res")
    mx, mz, mc = res // 4, lax.rem(res // 2, 2), lax.rem(res, 2)

    def at(x, z, c):
        return (sec, x * 4 + z * 2 + c)

    other_core = at(mx, mz, 1 - mc)
    other_z = at(mx, 1 - mz, mc)

    def x_peer(d):
        x = lax.rem(mx + d, NX)
        return x, at(x, mz, mc)

    loads = [
        pltpu.make_async_copy(src, dst, in_sem.at[n])
        for n, (src, dst) in enumerate(
            [(gain_hbm, gain), (nrm_hbm, nrm), (w1_hbm, w1), (w2_hbm, w2), (wout_hbm, wout)]
        )
    ]
    for load in loads:
        load.start()

    barrier = pltpu.get_barrier_semaphore()

    def greet(d, _):
        pl.semaphore_signal(
            barrier, inc=1, device_id=(lax.rem(sec + d, NSEC), res), device_id_type=MESH
        )
        return 0

    lax.fori_loop(1, NSEC, greet, 0)
    pl.semaphore_signal(barrier, inc=1, device_id=other_core, device_id_type=MESH)
    pl.semaphore_signal(barrier, inc=1, device_id=other_z, device_id_type=MESH)
    for d in range(1, NX):
        pl.semaphore_signal(barrier, inc=1, device_id=x_peer(d)[1], device_id_type=MESH)
    loads[0].wait()
    gsend[...] = jnp.broadcast_to(gain[...], gsend.shape)
    gall[sec] = gsend[...]
    pl.semaphore_wait(barrier, NSEC - 1 + 2 + NX - 1)

    def fwd(c, d):
        peer = lax.rem(sec + d, NSEC)
        return pltpu.make_async_remote_copy(
            src_ref=pext_hbm.at[peer, :, c],
            dst_ref=fr.at[c, sec],
            send_sem=fs_sem.at[c, d],
            recv_sem=fr_sem.at[c, sec],
            device_id=(peer, res),
            device_id_type=MESH,
        )

    def gains(d):
        peer = lax.rem(sec + d, NSEC)
        return pltpu.make_async_remote_copy(
            src_ref=gsend,
            dst_ref=gall.at[sec],
            send_sem=gs_sem.at[d],
            recv_sem=gr_sem.at[sec],
            device_id=(peer, res),
            device_id_type=MESH,
        )

    def each(body, low=1, high=NSEC):
        def step(d, _):
            body(d)
            return 0

        lax.fori_loop(low, high, step, 0, unroll=True)

    def send_fwd(c):
        each(lambda d: fwd(c, d).start())
        pltpu.make_async_copy(pext_hbm.at[sec, :, c], fr.at[c, sec], fr_sem.at[c, sec]).start()

    send_fwd(0)
    each(lambda d: gains(d).start())
    send_fwd(1)
    send_fwd(2)
    send_fwd(3)

    loads[1].wait()
    loads[2].wait()
    loads[3].wait()
    wt[:W] = w1[...]
    wt[W:] = w2[...]

    def project(n, _):
        block = nrm[pl.ds(n * 2, 2)].reshape(2 * SEQ, CH)
        both = lax.dot_general(
            wt[...], block, (((1,), (1,)), ((), ())), preferred_element_type=F32
        )
        for t in range(2):
            rows = pl.multiple_of((n * 2 + t) * W, W)
            lf[pl.ds(rows, W), :] = both[:W, t * SEQ : (t + 1) * SEQ]
            rf[pl.ds(rows, W), :] = both[W:, t * SEQ : (t + 1) * SEQ]
        return 0

    lax.fori_loop(0, ROWS // 2, project, 0, unroll=4)
    for y in range(W):
        rall[mx, mz, mc, y] = rf[pl.ds(y, ROWS, stride=W), :].astype(BF)

    def share(n, x, z, c, to):
        return pltpu.make_async_remote_copy(
            src_ref=rall.at[x, z, c],
            dst_ref=rall.at[x, z, c],
            send_sem=as_sem.at[n],
            recv_sem=ar_sem.at[x, z, c],
            device_id=to,
            device_id_type=MESH,
        )

    def arrived(x, z, c):
        pltpu.make_async_copy(rall.at[x, z, c], rall.at[x, z, c], ar_sem.at[x, z, c]).wait()

    shares = []

    def pass_on(copies):
        for copy in copies:
            copy.start()
        shares.extend(copies)

    pass_on(
        [share(0, mx, mz, mc, other_z)]
        + [share(d, mx, mz, mc, x_peer(d)[1]) for d in range(1, NX)]
        + [share(4, mx, mz, mc, other_core)]
    )

    for n in range(4):
        lt[:, n * 128 : (n + 1) * 128] = lf[n * 128 : (n + 1) * 128, :].T.astype(BF)
    loads[4].wait()
    wf[...] = wout[...].astype(F32)
    for y in range(W):
        wp[(y // 2) * W : (y // 2 + 1) * W, (y % 2) * PC : (y % 2 + 1) * PC] = wf[
            pl.ds(y, W, stride=W), :
        ].astype(BF)
    lacc[...] = jnp.zeros_like(lacc)

    def pass_z():
        arrived(mx, 1 - mz, mc)
        pass_on(
            [share(4 + d, mx, 1 - mz, mc, x_peer(d)[1]) for d in range(1, NX)]
            + [share(8, mx, 1 - mz, mc, other_core)]
        )

    def pass_x(n):
        for d in range(1, NX):
            x = x_peer(d)[0]
            z = mz if n == 0 else 1 - mz
            arrived(x, z, mc)
            pass_on([share(7 + 2 * d + n, x, z, mc, other_core)])

    def back(c, d):
        peer = lax.rem(sec + d, NSEC)
        return pltpu.make_async_remote_copy(
            src_ref=bs.at[c, peer],
            dst_ref=ph.at[c, sec],
            send_sem=bs_sem.at[c, d],
            recv_sem=br_sem.at[c, sec],
            device_id=(peer, res),
            device_id_type=MESH,
        )

    def gain_arrived(d):
        k = lax.rem(sec + d, NSEC)
        pltpu.make_async_copy(gall.at[k], gall.at[k], gr_sem.at[k]).wait()

    def scan(c):
        if c == 0:
            each(gain_arrived)
        each(lambda k: pltpu.make_async_copy(fr.at[c, k], fr.at[c, k], fr_sem.at[c, k]).wait(), 0)
        total = None
        for k in range(NSEC - 1, -1, -1):
            grad = fr[c, k].reshape(JC, PC).astype(F32)
            total = grad if total is None else grad + gall[k + 1, 0:1, :] * total
            bs[c, k] = total.astype(BF).reshape(NX, ROWS, PC)
        pltpu.make_async_copy(bs.at[c, sec], ph.at[c, sec], br_sem.at[c, sec]).start()
        each(lambda d: back(c, d).start())

    def core_copy(c, g):
        ys = pl.ds(g * YN, YN)
        return pltpu.make_async_remote_copy(
            src_ref=rg.at[c, :, ys],
            dst_ref=c1.at[c // 2, :, ys],
            send_sem=cs_sem.at[c, g],
            recv_sem=cr_sem.at[c // 2, g],
            device_id=other_core,
            device_id_type=MESH,
        )

    def x_copy(c, g, d):
        ys = pl.ds(g * YN, YN)
        x, peer = x_peer(d)
        return pltpu.make_async_remote_copy(
            src_ref=xs.at[c // 2, x, ys],
            dst_ref=xr.at[c // 2, mx, ys],
            send_sem=xs_sem.at[c // 2, g, d],
            recv_sem=xr_sem.at[c // 2, g, mx],
            device_id=peer,
            device_id_type=MESH,
        )

    def z_copy(g):
        ys = pl.ds(g * YN, YN)
        return pltpu.make_async_remote_copy(
            src_ref=zs.at[1 - mz, ys],
            dst_ref=zr.at[ys],
            send_sem=zs_sem.at[g],
            recv_sem=zr_sem.at[g],
            device_id=other_z,
            device_id_type=MESH,
        )

    def products(c):
        def outer(n, _):
            rows = [lax.rem(sec - n * 4 - t + NSEC, NSEC) for t in range(4)]
            for i in rows:
                pltpu.make_async_copy(ph.at[c, i], ph.at[c, i], br_sem.at[c, i]).wait()
            for two in (rows[:2], rows[2:]):
                wide = []
                for i in two:
                    pair = ph[c, i].reshape(JC, PC)
                    none = jnp.zeros_like(pair)
                    wide += [
                        jnp.concatenate([pair, none], axis=1),
                        jnp.concatenate([none, pair], axis=1),
                    ]
                grad = lax.dot_general(
                    wp[...],
                    jnp.concatenate(wide, axis=0),
                    (((1,), (1,)), ((), ())),
                    preferred_element_type=F32,
                ).astype(BF)
                for t, i in enumerate(two):
                    osc[c, i] = grad[:, t * 2 * JC : (t + 1) * 2 * JC].reshape(YP, W, 2 * JC)
            return 0

        lax.fori_loop(0, ROWS // 4, outer, 0)

        for g in range(YG):

            def right(n, _):
                for h in range(2):
                    yp = g * (YN // 2) + n * 4 + h * 2
                    both = jnp.concatenate(
                        [osc[c, :, yp + t].reshape(ROWS * W, 2 * JC) for t in range(2)], axis=1
                    )
                    grad = jnp.dot(lt[...], both, preferred_element_type=F32)
                    for t in range(2):
                        turned = grad[:, t * 2 * JC : (t + 1) * 2 * JC].T.astype(BF)
                        turned = turned.reshape(2, NX, ROWS, SEQ)
                        for u in range(2):
                            rg[c, :, (yp + t) * 2 + u] = turned[u]
                return 0

            lax.fori_loop(0, YN // 8, right, 0)

            @pl.when(mc != c % 2)
            def _():
                core_copy(c, g).start()

    def left_products(c):
        def left(n, _):
            terms = jnp.concatenate(
                [osc[c, :, n * 8 + t].reshape(ROWS * W, 2 * JC) for t in range(8)], axis=1
            )
            vectors = jnp.concatenate(
                [rall[:, c // 2, c % 2, n * 16 + t].reshape(JC, SEQ) for t in range(16)], axis=0
            )
            lacc[...] += jnp.dot(terms, vectors, preferred_element_type=F32)
            return 0

        lax.fori_loop(0, YP // 8, left, 0)

    def over_cores(c):
        @pl.when(mc == c % 2)
        def _():
            for g in range(YG):
                core_copy(c, g).wait_recv()

                def add_core(n, _):
                    y = g * YN + n
                    xs[c // 2, :, y] = (
                        rg[c, :, y].astype(F32) + c1[c // 2, :, y].astype(F32)
                    ).astype(BF)
                    return 0

                lax.fori_loop(0, YN, add_core, 0, unroll=4)
                for d in range(1, NX):
                    x_copy(c, g, d).start()

    def over_x(c):
        @pl.when(mc == c % 2)
        def _():
            for g in range(YG):
                for d in range(1, NX):
                    x = x_peer(d)[0]
                    part = xr.at[c // 2, x, pl.ds(g * YN, YN)]
                    pltpu.make_async_copy(part, part, xr_sem.at[c // 2, g, x]).wait()

                def add_x(n, _):
                    y = g * YN + n
                    total = xs[c // 2, mx, y].astype(F32)
                    for d in range(1, NX):
                        total += xr[c // 2, x_peer(d)[0], y].astype(F32)
                    zs[c // 2, y] = total.astype(BF)
                    return 0

                lax.fori_loop(0, YN, add_x, 0, unroll=4)

                @pl.when(mz != c // 2)
                def _():
                    z_copy(g).start()

    def over_z():
        for g in range(YG):
            z_copy(g).wait_recv()

            def add_z(n, _):
                y = g * YN + n
                rows = pl.multiple_of(y * ROWS, ROWS)
                rgf[pl.ds(rows, ROWS), :] = zs[mz, y].astype(F32) + zr[y].astype(F32)
                return 0

            lax.fori_loop(0, YN, add_z, 0, unroll=8)

    def sent_fwd():
        for c in range(NQ):
            each(lambda d: fwd(c, d).wait_send())
        each(lambda d: gains(d).wait_send())

    def sent_back():
        for c in range(NQ):
            each(lambda d: back(c, d).wait_send())
        for copy in shares:
            copy.wait_send()

    def sent(c):
        @pl.when(mc != c % 2)
        def _():
            for g in range(YG):
                core_copy(c, g).wait_send()

        @pl.when(mc == c % 2)
        def _():
            for g in range(YG):
                for d in range(1, NX):
                    x_copy(c, g, d).wait_send()

    def sent_z():
        for g in range(YG):
            z_copy(g).wait_send()

    scan(0)
    scan(1)
    scan(2)
    scan(3)
    pass_z()
    products(0)
    pass_x(0)
    over_cores(0)
    products(1)
    pass_x(1)
    over_x(0)
    over_cores(1)
    products(2)
    over_x(1)
    over_cores(2)
    sent_fwd()
    products(3)
    over_x(2)
    over_cores(3)
    for x in range(NX):
        for z in range(NZ):
            arrived(x, z, 1 - mc)
    left_products(0)
    left_products(1)
    left_products(2)
    left_products(3)
    for i in range(ROWS):
        lrv[i, :W] = (lacc[i * W : (i + 1) * W, :] * (1.0 / SEQ)).astype(BF)
    sent(0)
    sent(1)
    sent(2)
    sent_back()
    over_x(NQ - 1)
    over_z()

    for i in range(ROWS):
        lrv[i, W:] = (rgf[pl.ds(i, W, stride=ROWS), :] * (1.0 / SEQ)).astype(BF)
    done = pltpu.make_async_copy(lrv, lr_hbm, out_sem)
    done.start()
    sent(3)
    sent_z()

    done.wait()


def project_out(lr, w1, w2, out):
    weights = jnp.concatenate([w1[...], w2[...]], axis=0)
    for t in range(STEP):
        out[t] = lax.dot_general(
            lr[t], weights, (((0,), (0,)), ((), ())), preferred_element_type=F32
        ).astype(BF)


def shards(nrm, w1, w2, wout, pext, gain):
    anyspace = pl.BlockSpec(memory_space=pl.ANY)
    vm = pltpu.VMEM
    dma = pltpu.SemaphoreType.DMA
    w1t = jnp.swapaxes(w1[0], 0, 1)
    w2t = jnp.swapaxes(w2[0], 0, 1)
    lr = pl.pallas_call(
        kernel,
        out_shape=jax.ShapeDtypeStruct((ROWS, 2 * W, SEQ), BF),
        in_specs=[anyspace] * 6,
        out_specs=anyspace,
        scratch_shapes=[
            vm((ROWS, SEQ, CH), BF),
            vm((W, CH), BF),
            vm((W, CH), BF),
            vm((W * W, PC), BF),
            vm((1, PC), F32),
            vm((8, PC), F32),
            vm((NSEC, 8, PC), F32),
            vm((NQ, NSEC, NX, ROWS, PC), BF),
            vm((NQ, NSEC, NX, ROWS, PC), BF),
            vm((NQ, NSEC, NX, ROWS, PC), BF),
            vm((W * W, PC), F32),
            vm((YP * W, 2 * PC), BF),
            vm((ROWS * W, SEQ), F32),
            vm((SEQ, ROWS * W), BF),
            vm((ROWS * W, SEQ), F32),
            vm((NX, NZ, NC, W, ROWS, SEQ), BF),
            vm((NQ, ROWS, YP, W, 2 * JC), BF),
            vm((ROWS * W, SEQ), F32),
            vm((NQ, NX, W, ROWS, SEQ), BF),
            vm((2, NX, W, ROWS, SEQ), BF),
            vm((2, NX, W, ROWS, SEQ), BF),
            vm((2, NX, W, ROWS, SEQ), BF),
            vm((2, W, ROWS, SEQ), BF),
            vm((W, ROWS, SEQ), BF),
            vm((W * ROWS, SEQ), F32),
            vm((2 * W, CH), BF),
            vm((ROWS, 2 * W, SEQ), BF),
            dma((5,)),
            dma((NSEC,)),
            dma((NSEC,)),
            dma((NQ, NSEC)),
            dma((NQ, NSEC)),
            dma((NQ, NSEC)),
            dma((NQ, NSEC)),
            dma((16,)),
            dma((NX, NZ, NC)),
            dma((NQ, YG)),
            dma((NZ, YG)),
            dma((NZ, YG, NX)),
            dma((NZ, YG, NX)),
            dma((YG,)),
            dma((YG,)),
            dma,
        ],
        compiler_params=pltpu.CompilerParams(
            collective_id=0, has_side_effects=True, vmem_limit_bytes=56 << 20
        ),
        cost_estimate=pl.CostEstimate(
            flops=3_400_000_000, bytes_accessed=4 << 20, transcendentals=0
        ),
        name="fused",
    )(
        nrm[0],
        w1t,
        w2t,
        wout[0],
        pext[0].reshape(ROWS, NX, NQ, ROWS, PC),
        gain,
    )
    out = pl.pallas_call(
        project_out,
        out_shape=jax.ShapeDtypeStruct((ROWS, SEQ, CH), BF),
        grid=(ROWS // STEP,),
        in_specs=[
            pl.BlockSpec((STEP, 2 * W, SEQ), lambda n: (n, 0, 0)),
            pl.BlockSpec((W, CH), lambda n: (0, 0)),
            pl.BlockSpec((W, CH), lambda n: (0, 0)),
        ],
        out_specs=pl.BlockSpec((STEP, SEQ, CH), lambda n: (n, 0, 0)),
        name="project_out",
    )(lr, w1t, w2t)
    return out[None]


def solution(mesh):
    in_specs = (
        P("section", "res", None, None),
        P("section", None, None),
        P("section", None, None),
        P("section", None, None),
        P("section", "res", None, None),
        P("section", None),
    )
    out_specs = P("section", "res", None, None)
    return jax.shard_map(shards, mesh=mesh, in_specs=in_specs, out_specs=out_specs, check_vma=False)
```

```python
import jax
import jax.numpy as jnp
from jax import lax
from jax.experimental import pallas as pl
from jax.experimental.pallas import tpu as pltpu
from jax.sharding import PartitionSpec as P

MESH = pl.DeviceIdType.MESH
BF = jnp.bfloat16
F32 = jnp.float32
NSEC = 16
NRES = 16
ROWS = 16
SEQ = 128
CH = 256
W = 32
PC = 128
NX, NZ, NC = 4, 2, 2
NQ = NZ * NC
JC = NX * ROWS
YP = W // 2
YG = 4
YN = W // YG
STEP = 16


def kernel(
    nrm_hbm, w1_hbm, w2_hbm, wout_hbm, pext_hbm, gain_hbm, lr_hbm,
    nrm, w1, w2, wout, gain, gsend, gall,
    fr, bs, ph, wf, wp, lf, lt, rf, rall, osc, lacc, rg, c1, xs, xr, zs, zr, rgf, wt, lrv,
    in_sem, gs_sem, gr_sem, fs_sem, fr_sem, bs_sem, br_sem, as_sem, ar_sem,
    cs_sem, cr_sem, xs_sem, xr_sem, zs_sem, zr_sem, out_sem,
):
    sec = lax.axis_index("section")
    res = lax.axis_index("res")
    mx, mz, mc = res // 4, lax.rem(res // 2, 2), lax.rem(res, 2)

    def at(x, z, c):
        return (sec, x * 4 + z * 2 + c)

    other_core = at(mx, mz, 1 - mc)
    other_z = at(mx, 1 - mz, mc)

    def x_peer(d):
        x = lax.rem(mx + d, NX)
        return x, at(x, mz, mc)

    loads = [
        pltpu.make_async_copy(src, dst, in_sem.at[n])
        for n, (src, dst) in enumerate(
            [(gain_hbm, gain), (nrm_hbm, nrm), (w1_hbm, w1), (w2_hbm, w2), (wout_hbm, wout)]
        )
    ]
    for load in loads:
        load.start()

    barrier = pltpu.get_barrier_semaphore()

    def greet(d, _):
        pl.semaphore_signal(
            barrier, inc=1, device_id=(lax.rem(sec + d, NSEC), res), device_id_type=MESH
        )
        return 0

    lax.fori_loop(1, NSEC, greet, 0)
    pl.semaphore_signal(barrier, inc=1, device_id=other_core, device_id_type=MESH)
    pl.semaphore_signal(barrier, inc=1, device_id=other_z, device_id_type=MESH)
    for d in range(1, NX):
        pl.semaphore_signal(barrier, inc=1, device_id=x_peer(d)[1], device_id_type=MESH)
    loads[0].wait()
    gsend[...] = jnp.broadcast_to(gain[...], gsend.shape)
    gall[sec] = gsend[...]
    pl.semaphore_wait(barrier, NSEC - 1 + 2 + NX - 1)

    def fwd(c, d):
        peer = lax.rem(sec + d, NSEC)
        return pltpu.make_async_remote_copy(
            src_ref=pext_hbm.at[peer, :, c],
            dst_ref=fr.at[c, sec],
            send_sem=fs_sem.at[c, d],
            recv_sem=fr_sem.at[c, sec],
            device_id=(peer, res),
            device_id_type=MESH,
        )

    def gains(d):
        peer = lax.rem(sec + d, NSEC)
        return pltpu.make_async_remote_copy(
            src_ref=gsend,
            dst_ref=gall.at[sec],
            send_sem=gs_sem.at[d],
            recv_sem=gr_sem.at[sec],
            device_id=(peer, res),
            device_id_type=MESH,
        )

    def each(body, low=1, high=NSEC):
        def step(d, _):
            body(d)
            return 0

        lax.fori_loop(low, high, step, 0, unroll=True)

    def send_fwd(c):
        each(lambda d: fwd(c, d).start())
        pltpu.make_async_copy(pext_hbm.at[sec, :, c], fr.at[c, sec], fr_sem.at[c, sec]).start()

    send_fwd(0)
    each(lambda d: gains(d).start())
    send_fwd(1)
    send_fwd(2)
    send_fwd(3)

    loads[1].wait()
    loads[2].wait()
    loads[3].wait()
    wt[:W] = w1[...]
    wt[W:] = w2[...]

    def project(n, _):
        block = nrm[pl.ds(n * 2, 2)].reshape(2 * SEQ, CH)
        both = lax.dot_general(
            wt[...], block, (((1,), (1,)), ((), ())), preferred_element_type=F32
        )
        for t in range(2):
            rows = pl.multiple_of((n * 2 + t) * W, W)
            lf[pl.ds(rows, W), :] = both[:W, t * SEQ : (t + 1) * SEQ]
            rf[pl.ds(rows, W), :] = both[W:, t * SEQ : (t + 1) * SEQ]
        return 0

    lax.fori_loop(0, ROWS // 2, project, 0, unroll=4)
    for y in range(W):
        rall[mx, mz, mc, y] = rf[pl.ds(y, ROWS, stride=W), :].astype(BF)

    def share(n, x, z, c, to):
        return pltpu.make_async_remote_copy(
            src_ref=rall.at[x, z, c],
            dst_ref=rall.at[x, z, c],
            send_sem=as_sem.at[n],
            recv_sem=ar_sem.at[x, z, c],
            device_id=to,
            device_id_type=MESH,
        )

    def arrived(x, z, c):
        pltpu.make_async_copy(rall.at[x, z, c], rall.at[x, z, c], ar_sem.at[x, z, c]).wait()

    shares = []

    def pass_on(copies):
        for copy in copies:
            copy.start()
        shares.extend(copies)

    pass_on(
        [share(0, mx, mz, mc, other_z)]
        + [share(d, mx, mz, mc, x_peer(d)[1]) for d in range(1, NX)]
        + [share(4, mx, mz, mc, other_core)]
    )

    for n in range(4):
        lt[:, n * 128 : (n + 1) * 128] = lf[n * 128 : (n + 1) * 128, :].T.astype(BF)
    loads[4].wait()
    wf[...] = wout[...].astype(F32)
    for y in range(W):
        wp[(y // 2) * W : (y // 2 + 1) * W, (y % 2) * PC : (y % 2 + 1) * PC] = wf[
            pl.ds(y, W, stride=W), :
        ].astype(BF)
    lacc[...] = jnp.zeros_like(lacc)

    def pass_z():
        arrived(mx, 1 - mz, mc)
        pass_on(
            [share(4 + d, mx, 1 - mz, mc, x_peer(d)[1]) for d in range(1, NX)]
            + [share(8, mx, 1 - mz, mc, other_core)]
        )

    def pass_x(n):
        for d in range(1, NX):
            x = x_peer(d)[0]
            z = mz if n == 0 else 1 - mz
            arrived(x, z, mc)
            pass_on([share(7 + 2 * d + n, x, z, mc, other_core)])

    def back(c, d):
        peer = lax.rem(sec + d, NSEC)
        return pltpu.make_async_remote_copy(
            src_ref=bs.at[c, peer],
            dst_ref=ph.at[c, sec],
            send_sem=bs_sem.at[c, d],
            recv_sem=br_sem.at[c, sec],
            device_id=(peer, res),
            device_id_type=MESH,
        )

    def gain_arrived(d):
        k = lax.rem(sec + d, NSEC)
        pltpu.make_async_copy(gall.at[k], gall.at[k], gr_sem.at[k]).wait()

    def scan(c):
        if c == 0:
            each(gain_arrived)
        each(lambda k: pltpu.make_async_copy(fr.at[c, k], fr.at[c, k], fr_sem.at[c, k]).wait(), 0)
        total = None
        for k in range(NSEC - 1, -1, -1):
            grad = fr[c, k].reshape(JC, PC).astype(F32)
            total = grad if total is None else grad + gall[k + 1, 0:1, :] * total
            bs[c, k] = total.astype(BF).reshape(NX, ROWS, PC)
        pltpu.make_async_copy(bs.at[c, sec], ph.at[c, sec], br_sem.at[c, sec]).start()
        each(lambda d: back(c, d).start())

    def core_copy(c, g):
        ys = pl.ds(g * YN, YN)
        return pltpu.make_async_remote_copy(
            src_ref=rg.at[c, :, ys],
            dst_ref=c1.at[c // 2, :, ys],
            send_sem=cs_sem.at[c, g],
            recv_sem=cr_sem.at[c // 2, g],
            device_id=other_core,
            device_id_type=MESH,
        )

    def x_copy(c, g, d):
        ys = pl.ds(g * YN, YN)
        x, peer = x_peer(d)
        return pltpu.make_async_remote_copy(
            src_ref=xs.at[c // 2, x, ys],
            dst_ref=xr.at[c // 2, mx, ys],
            send_sem=xs_sem.at[c // 2, g, d],
            recv_sem=xr_sem.at[c // 2, g, mx],
            device_id=peer,
            device_id_type=MESH,
        )

    def z_copy(g):
        ys = pl.ds(g * YN, YN)
        return pltpu.make_async_remote_copy(
            src_ref=zs.at[1 - mz, ys],
            dst_ref=zr.at[ys],
            send_sem=zs_sem.at[g],
            recv_sem=zr_sem.at[g],
            device_id=other_z,
            device_id_type=MESH,
        )

    def products(c):
        def outer(n, _):
            rows = [lax.rem(sec - n * 4 - t + NSEC, NSEC) for t in range(4)]
            for i in rows:
                pltpu.make_async_copy(ph.at[c, i], ph.at[c, i], br_sem.at[c, i]).wait()
            for two in (rows[:2], rows[2:]):
                wide = []
                for i in two:
                    pair = ph[c, i].reshape(JC, PC)
                    none = jnp.zeros_like(pair)
                    wide += [
                        jnp.concatenate([pair, none], axis=1),
                        jnp.concatenate([none, pair], axis=1),
                    ]
                grad = lax.dot_general(
                    wp[...],
                    jnp.concatenate(wide, axis=0),
                    (((1,), (1,)), ((), ())),
                    preferred_element_type=F32,
                ).astype(BF)
                for t, i in enumerate(two):
                    osc[c, i] = grad[:, t * 2 * JC : (t + 1) * 2 * JC].reshape(YP, W, 2 * JC)
            return 0

        lax.fori_loop(0, ROWS // 4, outer, 0)

        for g in range(YG):

            def right(n, _):
                for h in range(2):
                    yp = g * (YN // 2) + n * 4 + h * 2
                    both = jnp.concatenate(
                        [osc[c, :, yp + t].reshape(ROWS * W, 2 * JC) for t in range(2)], axis=1
                    )
                    grad = jnp.dot(lt[...], both, preferred_element_type=F32)
                    for t in range(2):
                        turned = grad[:, t * 2 * JC : (t + 1) * 2 * JC].T.astype(BF)
                        turned = turned.reshape(2, NX, ROWS, SEQ)
                        for u in range(2):
                            rg[c, :, (yp + t) * 2 + u] = turned[u]
                return 0

            lax.fori_loop(0, YN // 8, right, 0)

            @pl.when(mc != c % 2)
            def _():
                core_copy(c, g).start()

    def left_products(c):
        def left(n, _):
            terms = jnp.concatenate(
                [osc[c, :, n * 8 + t].reshape(ROWS * W, 2 * JC) for t in range(8)], axis=1
            )
            vectors = jnp.concatenate(
                [rall[:, c // 2, c % 2, n * 16 + t].reshape(JC, SEQ) for t in range(16)], axis=0
            )
            lacc[...] += jnp.dot(terms, vectors, preferred_element_type=F32)
            return 0

        lax.fori_loop(0, YP // 8, left, 0)

    def over_cores(c):
        @pl.when(mc == c % 2)
        def _():
            for g in range(YG):
                core_copy(c, g).wait_recv()

                def add_core(n, _):
                    y = g * YN + n
                    xs[c // 2, :, y] = (
                        rg[c, :, y].astype(F32) + c1[c // 2, :, y].astype(F32)
                    ).astype(BF)
                    return 0

                lax.fori_loop(0, YN, add_core, 0, unroll=4)
                for d in range(1, NX):
                    x_copy(c, g, d).start()

    def over_x(c):
        @pl.when(mc == c % 2)
        def _():
            for g in range(YG):
                for d in range(1, NX):
                    x = x_peer(d)[0]
                    part = xr.at[c // 2, x, pl.ds(g * YN, YN)]
                    pltpu.make_async_copy(part, part, xr_sem.at[c // 2, g, x]).wait()

                def add_x(n, _):
                    y = g * YN + n
                    total = xs[c // 2, mx, y].astype(F32)
                    for d in range(1, NX):
                        total += xr[c // 2, x_peer(d)[0], y].astype(F32)
                    zs[c // 2, y] = total.astype(BF)
                    return 0

                lax.fori_loop(0, YN, add_x, 0, unroll=4)

                @pl.when(mz != c // 2)
                def _():
                    z_copy(g).start()

    def over_z():
        for g in range(YG):
            z_copy(g).wait_recv()

            def add_z(n, _):
                y = g * YN + n
                rows = pl.multiple_of(y * ROWS, ROWS)
                rgf[pl.ds(rows, ROWS), :] = zs[mz, y].astype(F32) + zr[y].astype(F32)
                return 0

            lax.fori_loop(0, YN, add_z, 0, unroll=8)

    def sent_fwd():
        for c in range(NQ):
            each(lambda d: fwd(c, d).wait_send())
        each(lambda d: gains(d).wait_send())

    def sent_back():
        for c in range(NQ):
            each(lambda d: back(c, d).wait_send())
        for copy in shares:
            copy.wait_send()

    def sent(c):
        @pl.when(mc != c % 2)
        def _():
            for g in range(YG):
                core_copy(c, g).wait_send()

        @pl.when(mc == c % 2)
        def _():
            for g in range(YG):
                for d in range(1, NX):
                    x_copy(c, g, d).wait_send()

    def sent_z():
        for g in range(YG):
            z_copy(g).wait_send()

    scan(0)
    scan(1)
    scan(2)
    scan(3)
    pass_z()
    products(0)
    pass_x(0)
    over_cores(0)
    products(1)
    pass_x(1)
    over_x(0)
    over_cores(1)
    products(2)
    over_x(1)
    over_cores(2)
    sent_fwd()
    products(3)
    over_cores(3)
    over_x(2)
    for x in range(NX):
        for z in range(NZ):
            arrived(x, z, 1 - mc)
    left_products(0)
    left_products(1)
    left_products(2)
    left_products(3)
    for i in range(ROWS):
        lrv[i, :W] = (lacc[i * W : (i + 1) * W, :] * (1.0 / SEQ)).astype(BF)
    over_x(NQ - 1)
    over_z()

    for i in range(ROWS):
        lrv[i, W:] = (rgf[pl.ds(i, W, stride=ROWS), :] * (1.0 / SEQ)).astype(BF)
    done = pltpu.make_async_copy(lrv, lr_hbm, out_sem)
    done.start()
    sent(0)
    sent(1)
    sent(2)
    sent_back()
    sent(3)
    sent_z()

    done.wait()


def project_out(lr, w1, w2, out):
    weights = jnp.concatenate([w1[...], w2[...]], axis=0)
    for t in range(STEP):
        out[t] = lax.dot_general(
            lr[t], weights, (((0,), (0,)), ((), ())), preferred_element_type=F32
        ).astype(BF)


def shards(nrm, w1, w2, wout, pext, gain):
    anyspace = pl.BlockSpec(memory_space=pl.ANY)
    vm = pltpu.VMEM
    dma = pltpu.SemaphoreType.DMA
    w1t = jnp.swapaxes(w1[0], 0, 1)
    w2t = jnp.swapaxes(w2[0], 0, 1)
    lr = pl.pallas_call(
        kernel,
        out_shape=jax.ShapeDtypeStruct((ROWS, 2 * W, SEQ), BF),
        in_specs=[anyspace] * 6,
        out_specs=anyspace,
        scratch_shapes=[
            vm((ROWS, SEQ, CH), BF),
            vm((W, CH), BF),
            vm((W, CH), BF),
            vm((W * W, PC), BF),
            vm((1, PC), F32),
            vm((8, PC), F32),
            vm((NSEC, 8, PC), F32),
            vm((NQ, NSEC, NX, ROWS, PC), BF),
            vm((NQ, NSEC, NX, ROWS, PC), BF),
            vm((NQ, NSEC, NX, ROWS, PC), BF),
            vm((W * W, PC), F32),
            vm((YP * W, 2 * PC), BF),
            vm((ROWS * W, SEQ), F32),
            vm((SEQ, ROWS * W), BF),
            vm((ROWS * W, SEQ), F32),
            vm((NX, NZ, NC, W, ROWS, SEQ), BF),
            vm((NQ, ROWS, YP, W, 2 * JC), BF),
            vm((ROWS * W, SEQ), F32),
            vm((NQ, NX, W, ROWS, SEQ), BF),
            vm((2, NX, W, ROWS, SEQ), BF),
            vm((2, NX, W, ROWS, SEQ), BF),
            vm((2, NX, W, ROWS, SEQ), BF),
            vm((2, W, ROWS, SEQ), BF),
            vm((W, ROWS, SEQ), BF),
            vm((W * ROWS, SEQ), F32),
            vm((2 * W, CH), BF),
            vm((ROWS, 2 * W, SEQ), BF),
            dma((5,)),
            dma((NSEC,)),
            dma((NSEC,)),
            dma((NQ, NSEC)),
            dma((NQ, NSEC)),
            dma((NQ, NSEC)),
            dma((NQ, NSEC)),
            dma((16,)),
            dma((NX, NZ, NC)),
            dma((NQ, YG)),
            dma((NZ, YG)),
            dma((NZ, YG, NX)),
            dma((NZ, YG, NX)),
            dma((YG,)),
            dma((YG,)),
            dma,
        ],
        compiler_params=pltpu.CompilerParams(
            collective_id=0, has_side_effects=True, vmem_limit_bytes=56 << 20
        ),
        cost_estimate=pl.CostEstimate(
            flops=3_400_000_000, bytes_accessed=4 << 20, transcendentals=0
        ),
        name="fused",
    )(
        nrm[0],
        w1t,
        w2t,
        wout[0],
        pext[0].reshape(ROWS, NX, NQ, ROWS, PC),
        gain,
    )
    out = pl.pallas_call(
        project_out,
        out_shape=jax.ShapeDtypeStruct((ROWS, SEQ, CH), BF),
        grid=(ROWS // STEP,),
        in_specs=[
            pl.BlockSpec((STEP, 2 * W, SEQ), lambda n: (n, 0, 0)),
            pl.BlockSpec((W, CH), lambda n: (0, 0)),
            pl.BlockSpec((W, CH), lambda n: (0, 0)),
        ],
        out_specs=pl.BlockSpec((STEP, SEQ, CH), lambda n: (n, 0, 0)),
        name="project_out",
    )(lr, w1t, w2t)
    return out[None]


def solution(mesh):
    in_specs = (
        P("section", "res", None, None),
        P("section", None, None),
        P("section", None, None),
        P("section", None, None),
        P("section", "res", None, None),
        P("section", None),
    )
    out_specs = P("section", "res", None, None)
    return jax.shard_map(shards, mesh=mesh, in_specs=in_specs, out_specs=out_specs, check_vma=False)
```

```python
import jax
import jax.numpy as jnp
from jax import lax
from jax.experimental import pallas as pl
from jax.experimental.pallas import tpu as pltpu
from jax.sharding import PartitionSpec as P

MESH = pl.DeviceIdType.MESH
BF = jnp.bfloat16
F32 = jnp.float32
NSEC = 16
NRES = 16
ROWS = 16
SEQ = 128
CH = 256
W = 32
PC = 128
NX, NZ, NC = 4, 2, 2
NQ = NZ * NC
JC = NX * ROWS
YP = W // 2
YG = 2
YN = W // YG
STEP = 16


def kernel(
    nrm_hbm, w1_hbm, w2_hbm, wout_hbm, pext_hbm, gain_hbm, lr_hbm,
    nrm, w1, w2, wout, gain, gsend, gall,
    fr, bs, ph, wf, wp, lf, lt, rf, rall, osc, lacc, rg, c1, xs, xr, zs, zr, rgf, wt, lrv,
    in_sem, gs_sem, gr_sem, fs_sem, fr_sem, bs_sem, br_sem, as_sem, ar_sem,
    cs_sem, cr_sem, xs_sem, xr_sem, zs_sem, zr_sem, out_sem,
):
    sec = lax.axis_index("section")
    res = lax.axis_index("res")
    mx, mz, mc = res // 4, lax.rem(res // 2, 2), lax.rem(res, 2)

    def at(x, z, c):
        return (sec, x * 4 + z * 2 + c)

    other_core = at(mx, mz, 1 - mc)
    other_z = at(mx, 1 - mz, mc)

    def x_peer(d):
        x = lax.rem(mx + d, NX)
        return x, at(x, mz, mc)

    loads = [
        pltpu.make_async_copy(src, dst, in_sem.at[n])
        for n, (src, dst) in enumerate(
            [(gain_hbm, gain), (nrm_hbm, nrm), (w1_hbm, w1), (w2_hbm, w2), (wout_hbm, wout)]
        )
    ]
    for load in loads:
        load.start()

    barrier = pltpu.get_barrier_semaphore()

    def greet(d, _):
        pl.semaphore_signal(
            barrier, inc=1, device_id=(lax.rem(sec + d, NSEC), res), device_id_type=MESH
        )
        return 0

    lax.fori_loop(1, NSEC, greet, 0)
    pl.semaphore_signal(barrier, inc=1, device_id=other_core, device_id_type=MESH)
    pl.semaphore_signal(barrier, inc=1, device_id=other_z, device_id_type=MESH)
    for d in range(1, NX):
        pl.semaphore_signal(barrier, inc=1, device_id=x_peer(d)[1], device_id_type=MESH)
    loads[0].wait()
    gsend[...] = jnp.broadcast_to(gain[...], gsend.shape)
    gall[sec] = gsend[...]
    pl.semaphore_wait(barrier, NSEC - 1 + 2 + NX - 1)

    def fwd(c, d):
        peer = lax.rem(sec + d, NSEC)
        return pltpu.make_async_remote_copy(
            src_ref=pext_hbm.at[peer, :, c],
            dst_ref=fr.at[c, sec],
            send_sem=fs_sem.at[c, d],
            recv_sem=fr_sem.at[c, sec],
            device_id=(peer, res),
            device_id_type=MESH,
        )

    def gains(d):
        peer = lax.rem(sec + d, NSEC)
        return pltpu.make_async_remote_copy(
            src_ref=gsend,
            dst_ref=gall.at[sec],
            send_sem=gs_sem.at[d],
            recv_sem=gr_sem.at[sec],
            device_id=(peer, res),
            device_id_type=MESH,
        )

    def each(body, low=1, high=NSEC):
        def step(d, _):
            body(d)
            return 0

        lax.fori_loop(low, high, step, 0, unroll=True)

    def send_fwd(c):
        each(lambda d: fwd(c, d).start())
        pltpu.make_async_copy(pext_hbm.at[sec, :, c], fr.at[c, sec], fr_sem.at[c, sec]).start()

    send_fwd(0)
    each(lambda d: gains(d).start())
    send_fwd(1)
    send_fwd(2)
    send_fwd(3)

    loads[1].wait()
    loads[2].wait()
    loads[3].wait()
    wt[:W] = w1[...]
    wt[W:] = w2[...]

    def project(n, _):
        block = nrm[pl.ds(n * 2, 2)].reshape(2 * SEQ, CH)
        both = lax.dot_general(
            wt[...], block, (((1,), (1,)), ((), ())), preferred_element_type=F32
        )
        for t in range(2):
            rows = pl.multiple_of((n * 2 + t) * W, W)
            lf[pl.ds(rows, W), :] = both[:W, t * SEQ : (t + 1) * SEQ]
            rf[pl.ds(rows, W), :] = both[W:, t * SEQ : (t + 1) * SEQ]
        return 0

    lax.fori_loop(0, ROWS // 2, project, 0, unroll=4)
    for y in range(W):
        rall[mx, mz, mc, y] = rf[pl.ds(y, ROWS, stride=W), :].astype(BF)

    def share(n, x, z, c, to):
        return pltpu.make_async_remote_copy(
            src_ref=rall.at[x, z, c],
            dst_ref=rall.at[x, z, c],
            send_sem=as_sem.at[n],
            recv_sem=ar_sem.at[x, z, c],
            device_id=to,
            device_id_type=MESH,
        )

    def arrived(x, z, c):
        pltpu.make_async_copy(rall.at[x, z, c], rall.at[x, z, c], ar_sem.at[x, z, c]).wait()

    shares = []

    def pass_on(copies):
        for copy in copies:
            copy.start()
        shares.extend(copies)

    pass_on(
        [share(0, mx, mz, mc, other_z)]
        + [share(d, mx, mz, mc, x_peer(d)[1]) for d in range(1, NX)]
        + [share(4, mx, mz, mc, other_core)]
    )

    for n in range(4):
        lt[:, n * 128 : (n + 1) * 128] = lf[n * 128 : (n + 1) * 128, :].T.astype(BF)
    loads[4].wait()
    wf[...] = wout[...].astype(F32)
    for y in range(W):
        wp[(y // 2) * W : (y // 2 + 1) * W, (y % 2) * PC : (y % 2 + 1) * PC] = wf[
            pl.ds(y, W, stride=W), :
        ].astype(BF)
    lacc[...] = jnp.zeros_like(lacc)

    def pass_z():
        arrived(mx, 1 - mz, mc)
        pass_on(
            [share(4 + d, mx, 1 - mz, mc, x_peer(d)[1]) for d in range(1, NX)]
            + [share(8, mx, 1 - mz, mc, other_core)]
        )

    def pass_x(n):
        for d in range(1, NX):
            x = x_peer(d)[0]
            z = mz if n == 0 else 1 - mz
            arrived(x, z, mc)
            pass_on([share(7 + 2 * d + n, x, z, mc, other_core)])

    def back(c, d):
        peer = lax.rem(sec + d, NSEC)
        return pltpu.make_async_remote_copy(
            src_ref=bs.at[c, peer],
            dst_ref=ph.at[c, sec],
            send_sem=bs_sem.at[c, d],
            recv_sem=br_sem.at[c, sec],
            device_id=(peer, res),
            device_id_type=MESH,
        )

    def gain_arrived(d):
        k = lax.rem(sec + d, NSEC)
        pltpu.make_async_copy(gall.at[k], gall.at[k], gr_sem.at[k]).wait()

    def scan(c):
        if c == 0:
            each(gain_arrived)
        each(lambda k: pltpu.make_async_copy(fr.at[c, k], fr.at[c, k], fr_sem.at[c, k]).wait(), 0)
        total = None
        for k in range(NSEC - 1, -1, -1):
            grad = fr[c, k].reshape(JC, PC).astype(F32)
            total = grad if total is None else grad + gall[k + 1, 0:1, :] * total
            bs[c, k] = total.astype(BF).reshape(NX, ROWS, PC)
        pltpu.make_async_copy(bs.at[c, sec], ph.at[c, sec], br_sem.at[c, sec]).start()
        each(lambda d: back(c, d).start())

    def core_copy(c, g):
        ys = pl.ds(g * YN, YN)
        return pltpu.make_async_remote_copy(
            src_ref=rg.at[c, :, ys],
            dst_ref=c1.at[c // 2, :, ys],
            send_sem=cs_sem.at[c, g],
            recv_sem=cr_sem.at[c // 2, g],
            device_id=other_core,
            device_id_type=MESH,
        )

    def x_copy(c, g, d):
        ys = pl.ds(g * YN, YN)
        x, peer = x_peer(d)
        return pltpu.make_async_remote_copy(
            src_ref=xs.at[c // 2, x, ys],
            dst_ref=xr.at[c // 2, mx, ys],
            send_sem=xs_sem.at[c // 2, g, d],
            recv_sem=xr_sem.at[c // 2, g, mx],
            device_id=peer,
            device_id_type=MESH,
        )

    def z_copy(g):
        ys = pl.ds(g * YN, YN)
        return pltpu.make_async_remote_copy(
            src_ref=zs.at[1 - mz, ys],
            dst_ref=zr.at[ys],
            send_sem=zs_sem.at[g],
            recv_sem=zr_sem.at[g],
            device_id=other_z,
            device_id_type=MESH,
        )

    def products(c):
        def outer(n, _):
            rows = [lax.rem(sec - n * 4 - t + NSEC, NSEC) for t in range(4)]
            for i in rows:
                pltpu.make_async_copy(ph.at[c, i], ph.at[c, i], br_sem.at[c, i]).wait()
            for two in (rows[:2], rows[2:]):
                wide = []
                for i in two:
                    pair = ph[c, i].reshape(JC, PC)
                    none = jnp.zeros_like(pair)
                    wide += [
                        jnp.concatenate([pair, none], axis=1),
                        jnp.concatenate([none, pair], axis=1),
                    ]
                grad = lax.dot_general(
                    wp[...],
                    jnp.concatenate(wide, axis=0),
                    (((1,), (1,)), ((), ())),
                    preferred_element_type=F32,
                ).astype(BF)
                for t, i in enumerate(two):
                    osc[c, i] = grad[:, t * 2 * JC : (t + 1) * 2 * JC].reshape(YP, W, 2 * JC)
            return 0

        lax.fori_loop(0, ROWS // 4, outer, 0)

        for g in range(YG):

            def right(n, _):
                for h in range(2):
                    yp = g * (YN // 2) + n * 4 + h * 2
                    both = jnp.concatenate(
                        [osc[c, :, yp + t].reshape(ROWS * W, 2 * JC) for t in range(2)], axis=1
                    )
                    grad = jnp.dot(lt[...], both, preferred_element_type=F32)
                    for t in range(2):
                        turned = grad[:, t * 2 * JC : (t + 1) * 2 * JC].T.astype(BF)
                        turned = turned.reshape(2, NX, ROWS, SEQ)
                        for u in range(2):
                            rg[c, :, (yp + t) * 2 + u] = turned[u]
                return 0

            lax.fori_loop(0, YN // 8, right, 0)

            @pl.when(mc != c % 2)
            def _():
                core_copy(c, g).start()

    def left_products(c):
        def left(n, _):
            terms = jnp.concatenate(
                [osc[c, :, n * 8 + t].reshape(ROWS * W, 2 * JC) for t in range(8)], axis=1
            )
            vectors = jnp.concatenate(
                [rall[:, c // 2, c % 2, n * 16 + t].reshape(JC, SEQ) for t in range(16)], axis=0
            )
            lacc[...] += jnp.dot(terms, vectors, preferred_element_type=F32)
            return 0

        lax.fori_loop(0, YP // 8, left, 0)

    def over_cores(c):
        @pl.when(mc == c % 2)
        def _():
            for g in range(YG):
                core_copy(c, g).wait_recv()

                def add_core(n, _):
                    y = g * YN + n
                    xs[c // 2, :, y] = (
                        rg[c, :, y].astype(F32) + c1[c // 2, :, y].astype(F32)
                    ).astype(BF)
                    return 0

                lax.fori_loop(0, YN, add_core, 0, unroll=4)
                for d in range(1, NX):
                    x_copy(c, g, d).start()

    def over_x(c):
        @pl.when(mc == c % 2)
        def _():
            for g in range(YG):
                for d in range(1, NX):
                    x = x_peer(d)[0]
                    part = xr.at[c // 2, x, pl.ds(g * YN, YN)]
                    pltpu.make_async_copy(part, part, xr_sem.at[c // 2, g, x]).wait()

                def add_x(n, _):
                    y = g * YN + n
                    total = xs[c // 2, mx, y].astype(F32)
                    for d in range(1, NX):
                        total += xr[c // 2, x_peer(d)[0], y].astype(F32)
                    zs[c // 2, y] = total.astype(BF)
                    return 0

                lax.fori_loop(0, YN, add_x, 0, unroll=4)

                @pl.when(mz != c // 2)
                def _():
                    z_copy(g).start()

    def over_z():
        for g in range(YG):
            z_copy(g).wait_recv()

            def add_z(n, _):
                y = g * YN + n
                rows = pl.multiple_of(y * ROWS, ROWS)
                rgf[pl.ds(rows, ROWS), :] = zs[mz, y].astype(F32) + zr[y].astype(F32)
                return 0

            lax.fori_loop(0, YN, add_z, 0, unroll=8)

    def sent_fwd():
        for c in range(NQ):
            each(lambda d: fwd(c, d).wait_send())
        each(lambda d: gains(d).wait_send())

    def sent_back():
        for c in range(NQ):
            each(lambda d: back(c, d).wait_send())
        for copy in shares:
            copy.wait_send()

    def sent(c):
        @pl.when(mc != c % 2)
        def _():
            for g in range(YG):
                core_copy(c, g).wait_send()

        @pl.when(mc == c % 2)
        def _():
            for g in range(YG):
                for d in range(1, NX):
                    x_copy(c, g, d).wait_send()

    def sent_z():
        for g in range(YG):
            z_copy(g).wait_send()

    scan(0)
    scan(1)
    scan(2)
    scan(3)
    pass_z()
    products(0)
    pass_x(0)
    over_cores(0)
    products(1)
    pass_x(1)
    over_x(0)
    over_cores(1)
    products(2)
    over_x(1)
    over_cores(2)
    sent_fwd()
    products(3)
    over_cores(3)
    over_x(2)
    for x in range(NX):
        for z in range(NZ):
            arrived(x, z, 1 - mc)
    left_products(0)
    left_products(1)
    left_products(2)
    left_products(3)
    for i in range(ROWS):
        lrv[i, :W] = (lacc[i * W : (i + 1) * W, :] * (1.0 / SEQ)).astype(BF)
    over_x(NQ - 1)
    over_z()

    for i in range(ROWS):
        lrv[i, W:] = (rgf[pl.ds(i, W, stride=ROWS), :] * (1.0 / SEQ)).astype(BF)
    done = pltpu.make_async_copy(lrv, lr_hbm, out_sem)
    done.start()
    sent(0)
    sent(1)
    sent(2)
    sent_back()
    sent(3)
    sent_z()

    done.wait()


def project_out(lr, w1, w2, out):
    weights = jnp.concatenate([w1[...], w2[...]], axis=0)
    for t in range(STEP):
        out[t] = lax.dot_general(
            lr[t], weights, (((0,), (0,)), ((), ())), preferred_element_type=F32
        ).astype(BF)


def shards(nrm, w1, w2, wout, pext, gain):
    anyspace = pl.BlockSpec(memory_space=pl.ANY)
    vm = pltpu.VMEM
    dma = pltpu.SemaphoreType.DMA
    w1t = jnp.swapaxes(w1[0], 0, 1)
    w2t = jnp.swapaxes(w2[0], 0, 1)
    lr = pl.pallas_call(
        kernel,
        out_shape=jax.ShapeDtypeStruct((ROWS, 2 * W, SEQ), BF),
        in_specs=[anyspace] * 6,
        out_specs=anyspace,
        scratch_shapes=[
            vm((ROWS, SEQ, CH), BF),
            vm((W, CH), BF),
            vm((W, CH), BF),
            vm((W * W, PC), BF),
            vm((1, PC), F32),
            vm((8, PC), F32),
            vm((NSEC, 8, PC), F32),
            vm((NQ, NSEC, NX, ROWS, PC), BF),
            vm((NQ, NSEC, NX, ROWS, PC), BF),
            vm((NQ, NSEC, NX, ROWS, PC), BF),
            vm((W * W, PC), F32),
            vm((YP * W, 2 * PC), BF),
            vm((ROWS * W, SEQ), F32),
            vm((SEQ, ROWS * W), BF),
            vm((ROWS * W, SEQ), F32),
            vm((NX, NZ, NC, W, ROWS, SEQ), BF),
            vm((NQ, ROWS, YP, W, 2 * JC), BF),
            vm((ROWS * W, SEQ), F32),
            vm((NQ, NX, W, ROWS, SEQ), BF),
            vm((2, NX, W, ROWS, SEQ), BF),
            vm((2, NX, W, ROWS, SEQ), BF),
            vm((2, NX, W, ROWS, SEQ), BF),
            vm((2, W, ROWS, SEQ), BF),
            vm((W, ROWS, SEQ), BF),
            vm((W * ROWS, SEQ), F32),
            vm((2 * W, CH), BF),
            vm((ROWS, 2 * W, SEQ), BF),
            dma((5,)),
            dma((NSEC,)),
            dma((NSEC,)),
            dma((NQ, NSEC)),
            dma((NQ, NSEC)),
            dma((NQ, NSEC)),
            dma((NQ, NSEC)),
            dma((16,)),
            dma((NX, NZ, NC)),
            dma((NQ, YG)),
            dma((NZ, YG)),
            dma((NZ, YG, NX)),
            dma((NZ, YG, NX)),
            dma((YG,)),
            dma((YG,)),
            dma,
        ],
        compiler_params=pltpu.CompilerParams(
            collective_id=0, has_side_effects=True, vmem_limit_bytes=56 << 20
        ),
        cost_estimate=pl.CostEstimate(
            flops=3_400_000_000, bytes_accessed=4 << 20, transcendentals=0
        ),
        name="fused",
    )(
        nrm[0],
        w1t,
        w2t,
        wout[0],
        pext[0].reshape(ROWS, NX, NQ, ROWS, PC),
        gain,
    )
    out = pl.pallas_call(
        project_out,
        out_shape=jax.ShapeDtypeStruct((ROWS, SEQ, CH), BF),
        grid=(ROWS // STEP,),
        in_specs=[
            pl.BlockSpec((STEP, 2 * W, SEQ), lambda n: (n, 0, 0)),
            pl.BlockSpec((W, CH), lambda n: (0, 0)),
            pl.BlockSpec((W, CH), lambda n: (0, 0)),
        ],
        out_specs=pl.BlockSpec((STEP, SEQ, CH), lambda n: (n, 0, 0)),
        name="project_out",
    )(lr, w1t, w2t)
    return out[None]


def solution(mesh):
    in_specs = (
        P("section", "res", None, None),
        P("section", None, None),
        P("section", None, None),
        P("section", None, None),
        P("section", "res", None, None),
        P("section", None),
    )
    out_specs = P("section", "res", None, None)
    return jax.shard_map(shards, mesh=mesh, in_specs=in_specs, out_specs=out_specs, check_vma=False)
```
